512 devices in a mesh: ctx: 128 (over z, x, y_lo), tp: 4 (over y_hi, core).
Axes of the slice: x: 4, y: 8 (y_hi: 2, y_lo: 4; y = y_hi * 4 + y_lo), z: 8, core: 2. Of those that a mesh axis runs over, the one named last changes fastest.
Arguments:
- self_queries: bfloat16 [16384, 8192], P('ctx', 'tp'), may hold values from -1000 to 1000
- cross_queries: bfloat16 [16384, 8192], P('ctx', 'tp'), may hold values from -1000 to 1000
- text_pairs: bfloat16 [2, 16384, 1024], P(None, 'ctx', 'tp'), may hold values from -4 to 4
- image_pairs: bfloat16 [2, 256, 128, 1024], P(None, 'ctx', 'tp'), may hold values from -4 to 4
- doc_lengths: int32 [64], replicated, may hold values from 1 to 385, 16384 in all
- image_places: int32 [256], replicated, may hold values from -1 to 16383, as said below
Outputs:
- self_out: bfloat16 [16384, 8192], P('ctx', 'tp')
- cross_out: bfloat16 [16384, 8192], P('ctx', 'tp')
The draws below stay inside these ranges and needn't reach their ends.
Inputs may be any that keep to these rules, and one draw needn't show every extreme that they name: `doc_lengths`: they sum to 16384; the longest document has exactly 385 tokens. `image_places`: entry s is -1 for an empty slot, else the position of its image in the token order, which lies in context block s // 2; the positions are distinct.
All inputs are finite; a program needn't handle non-finite values.
Results may differ from the reference program's by a relative error of at most 0.0054.
Values may be sent and summed in bfloat16 or wider, within the bound.
A program may use at most 64 MiB of HBM per device.

```python
import math
import jax
import jax.numpy as jnp
import numpy as np
from jax import lax

QUERY_HEADS = 64
KEY_VALUE_HEADS = 8
HEAD_DIM = 128
TOK_DEV = 128
IMAGE_TOKENS = 128
IMG_DEV = 2
SPAN = 4
TOKENS = 16384
SLOT_TOTAL = 256
NDOC = 64
MAXDOC = 385


def blended_table(key, shape):
    gaussian = jnp.clip(jax.random.normal(jax.random.fold_in(key, 1), shape, jnp.float32), -4.0, 4.0)
    return gaussian


def slot_layout(key):
    block_total = TOKENS // TOK_DEV
    part_width = TOK_DEV // IMG_DEV
    within = jax.random.randint(jax.random.fold_in(key, 31), (block_total, IMG_DEV), 0, part_width, jnp.int32)
    filled = jax.random.randint(jax.random.fold_in(key, 32), (block_total, IMG_DEV), 0, 4, jnp.int32)
    starts = jnp.arange(block_total, dtype=jnp.int32)[:, None] * TOK_DEV + jnp.arange(IMG_DEV, dtype=jnp.int32)[None, :] * part_width
    return jnp.where(filled > 0, starts + within, -1).reshape(-1).astype(jnp.int32)


def draw_image_places(key, part):
    return slot_layout(key)


def draw_text_pairs(key, part):
    paired_table = blended_table(jax.random.fold_in(key, 5), (2, TOKENS, KEY_VALUE_HEADS * HEAD_DIM))
    return paired_table.astype(jnp.bfloat16)


def draw_self_queries(key, part):
    own_key = jax.random.fold_in(key, 7)
    queries = blended_table(own_key, (TOKENS, QUERY_HEADS * HEAD_DIM))
    return queries.astype(jnp.bfloat16)


def draw_image_pairs(key, part):
    paired_table = blended_table(jax.random.fold_in(key, 6), (2, SLOT_TOTAL, IMAGE_TOKENS, KEY_VALUE_HEADS * HEAD_DIM))
    return paired_table.astype(jnp.bfloat16)


def draw_cross_queries(key, part):
    own_key = jax.random.fold_in(key, 8)
    queries = blended_table(own_key, (TOKENS, QUERY_HEADS * HEAD_DIM))
    return queries.astype(jnp.bfloat16)


def length_profile(number_of, total, bound, lean):
    loads = [(1 << 20) // math.isqrt(standing ** lean) + 1 for standing in range(2, number_of + 1)]
    rest, counts = total - bound - (number_of - 1), [1] * (number_of - 1)
    while rest > 0:
        free = [i for i in range(number_of - 1) if counts[i] < bound]
        pool, left = sum([loads[i] for i in free]), rest
        for i in free:
            addition = min(bound - counts[i], max(1, left * loads[i] // pool), rest)
            counts[i] = counts[i] + addition
            rest = rest - addition
    return np.array([bound] + counts)


def uneven(stream_key, amount, total, bound, skew):
    if amount == 2:
        one = jax.random.randint(stream_key, (), max(1, total - bound), min(bound, total - 1) + 1)
        return jnp.stack([one, total - one])
    sizes = jnp.asarray(length_profile(amount, total, bound, skew), jnp.int32)
    couples = (amount - 1) // 2
    source_of, receiver = sizes[1:1 + 2 * couples:2], sizes[2:2 + 2 * couples:2]
    room = jnp.minimum(source_of - 1, bound - receiver)
    passed = jax.random.randint(jax.random.fold_in(stream_key, 1), (couples,), 0, 1 << 20) % (room + 1)
    sizes = sizes.at[1:1 + 2 * couples:2].set(source_of - passed).at[2:2 + 2 * couples:2].set(receiver + passed)
    return sizes[jax.random.permutation(jax.random.fold_in(stream_key, 2), amount)]


def setup_inputs(seed: int = 0) -> dict:
    arg_keys = jax.random.split(jax.random.key(seed), 7)
    self_queries = draw_self_queries(jax.random.fold_in(arg_keys[6], 71), 0)
    cross_queries = draw_cross_queries(jax.random.fold_in(arg_keys[6], 71), 0)
    text_pairs = draw_text_pairs(jax.random.fold_in(arg_keys[6], 71), 0)
    image_pairs = draw_image_pairs(jax.random.fold_in(arg_keys[6], 71), 0)
    doc_lengths = uneven(arg_keys[4], NDOC, TOKENS, MAXDOC, 1).astype(jnp.int32)
    image_places = draw_image_places(jax.random.fold_in(arg_keys[6], 71), 0)
    return {"self_queries": self_queries, "cross_queries": cross_queries, "text_pairs": text_pairs, "image_pairs": image_pairs, "doc_lengths": doc_lengths, "image_places": image_places}


masked_score = -1e30


def fresh_state(row_count, group_count, head_ratio):
    return (jnp.full((row_count, group_count, head_ratio), masked_score, jnp.float32),
            jnp.zeros((row_count, group_count, head_ratio), jnp.float32),
            jnp.zeros((row_count, group_count, head_ratio, HEAD_DIM), jnp.float32))


def absorb(carried, queries, key_block, value_block, visible):
    running_max, running_sum, weighted = carried
    scores = jnp.einsum("tgrd,kgd->tgrk", queries.astype(jnp.float32), key_block.astype(jnp.float32))
    scores = scores * (HEAD_DIM ** -0.5)
    shown_mask = visible[:, None, None, :]
    scores = jnp.where(shown_mask, scores, masked_score)
    new_max = jnp.maximum(running_max, jnp.max(scores, axis=-1))
    weights = jnp.where(shown_mask, jnp.exp(scores - new_max[..., None]), 0.0)
    factor = jnp.exp(running_max - new_max)
    running_sum = running_sum * factor + jnp.sum(weights, axis=-1)
    rounded = lax.optimization_barrier(weights.astype(jnp.bfloat16)).astype(jnp.float32)
    product = jnp.einsum("tgrk,kgd->tgrd", rounded, value_block.astype(jnp.float32))
    weighted = weighted * factor[..., None] + product
    return new_max, running_sum, weighted


def finish(carried):
    running_max, running_sum, weighted = carried
    positive = running_sum > 0.0
    safe_sum = jnp.where(positive, running_sum, 1.0)
    result = jnp.where(positive[..., None], weighted / safe_sum[..., None], 0.0)
    return result.reshape(result.shape[0], -1).astype(jnp.bfloat16)


def reference(self_queries, cross_queries, text_pairs, image_pairs, doc_lengths, image_places):
    block_total = TOKENS // TOK_DEV
    head_ratio = QUERY_HEADS // KEY_VALUE_HEADS
    doc_ends = jnp.cumsum(doc_lengths).astype(jnp.int32)
    doc_starts = (doc_ends - doc_lengths).astype(jnp.int32)
    front_pad = (SPAN - 1) * TOK_DEV
    padded_text = jnp.concatenate([jnp.zeros((2, front_pad, KEY_VALUE_HEADS * HEAD_DIM), text_pairs.dtype), text_pairs], axis=1)
    padded_image = jnp.concatenate([jnp.zeros((2, (SPAN - 1) * IMG_DEV, IMAGE_TOKENS, KEY_VALUE_HEADS * HEAD_DIM), image_pairs.dtype), image_pairs], axis=1)
    padded_places = jnp.concatenate([jnp.full(((SPAN - 1) * IMG_DEV,), -1, jnp.int32), image_places.astype(jnp.int32)])
    offsets = jnp.arange(TOK_DEV, dtype=jnp.int32)
    window_offsets = jnp.arange(SPAN * TOK_DEV, dtype=jnp.int32)

    def one_block(block_index):
        places = block_index * TOK_DEV + offsets
        inside = (doc_starts[None, :] <= places[:, None]) & (places[:, None] < doc_ends[None, :])
        doc_begin = jnp.sum(jnp.where(inside, doc_starts[None, :], 0), axis=1).astype(jnp.int32)
        self_query = lax.dynamic_slice_in_dim(self_queries, block_index * TOK_DEV, TOK_DEV, 0).reshape(TOK_DEV, KEY_VALUE_HEADS, head_ratio, HEAD_DIM)
        cross_query = lax.dynamic_slice_in_dim(cross_queries, block_index * TOK_DEV, TOK_DEV, 0).reshape(TOK_DEV, KEY_VALUE_HEADS, head_ratio, HEAD_DIM)
        window = lax.dynamic_slice_in_dim(padded_text, block_index * TOK_DEV, SPAN * TOK_DEV, 1)
        key_places = (block_index - SPAN + 1) * TOK_DEV + window_offsets
        text_seen = (key_places[None, :] >= doc_begin[:, None]) & (key_places[None, :] <= places[:, None])
        self_state = absorb(fresh_state(TOK_DEV, KEY_VALUE_HEADS, head_ratio), self_query,
                            window[0].reshape(SPAN * TOK_DEV, KEY_VALUE_HEADS, HEAD_DIM), window[1].reshape(SPAN * TOK_DEV, KEY_VALUE_HEADS, HEAD_DIM), text_seen)
        image_window = lax.dynamic_slice_in_dim(padded_image, block_index * IMG_DEV, SPAN * IMG_DEV, 1)
        slot_places = lax.dynamic_slice_in_dim(padded_places, block_index * IMG_DEV, SPAN * IMG_DEV, 0)
        token_places = jnp.repeat(slot_places, IMAGE_TOKENS)
        image_seen = (token_places[None, :] >= doc_begin[:, None]) & (token_places[None, :] <= places[:, None])
        image_count = SPAN * IMG_DEV * IMAGE_TOKENS
        cross_state = absorb(fresh_state(TOK_DEV, KEY_VALUE_HEADS, head_ratio), cross_query,
                             image_window[0].reshape(image_count, KEY_VALUE_HEADS, HEAD_DIM), image_window[1].reshape(image_count, KEY_VALUE_HEADS, HEAD_DIM), image_seen)
        return finish(self_state), finish(cross_state)

    self_out, cross_out = lax.map(one_block, jnp.arange(block_total, dtype=jnp.int32))
    return self_out.reshape(TOKENS, QUERY_HEADS * HEAD_DIM), cross_out.reshape(TOKENS, QUERY_HEADS * HEAD_DIM)
```

```python
import functools
import math
import jax
import jax.numpy as jnp
from jax import lax
from jax.experimental import pallas as pl
from jax.experimental.pallas import tpu as pltpu
from jax.sharding import PartitionSpec as P

HEAD_DIM = 128
ROW = 4
OWN = 4
TEXT, NEAR, FAR = 0, 5, 10
HIDDEN = -1e30
LOWEST = -1e29
EXPONENT = math.log2(math.e) / math.sqrt(HEAD_DIM)
MESH = pl.DeviceIdType.MESH

ARRIVALS = (
    (TEXT, (1, 0, 1, 2), (0, 1, 1, 0)),
    (FAR, (3, 3, 0, 0), (1, 1, -1, -1)),
    (FAR, (2, 2, 1, 1), (1, -3, -1, -1)),
    (NEAR, (1, 0, 1, 2), (0, 1, 1, 0)),
    (TEXT, (2, 2, 3, 1), (0, -1, -1, 0)),
    (NEAR, (2, 2, 3, 1), (0, -1, -1, 0)),
    (FAR, (0, 0, 3, 3), (0, -1, -3, 0)),
    (TEXT, (3, 3, 0, 0), (0, -1, 1, 0)),
    (NEAR, (3, 3, 0, 0), (0, -1, 1, 0)),
    (FAR, (1, 1, 2, 2), (0, 3, 1, 0)),
)
FAR_STEP = (3, 2, 2, 1)


def pick(place, values):
    result = jnp.int32(values[-1])
    for index, value in enumerate(values[:-1]):
        result = jnp.where(place == index, value, result)
    return result


def attend(queries, chunks, bias, tops, totals, sums, kind, chunk, first):
    for group in range(2):
        columns = slice(group * HEAD_DIM, (group + 1) * HEAD_DIM)
        keys = chunks[chunk, 0, :, :, :, columns].reshape(HEAD_DIM, HEAD_DIM)
        values = chunks[chunk, 1, :, :, :, columns].reshape(HEAD_DIM, HEAD_DIM)
        heads = [queries[kind, :, h * HEAD_DIM : (h + 1) * HEAD_DIM] for h in range(group * 8, group * 8 + 8)]
        stacked = jnp.concatenate(heads, axis=0)
        scores = lax.dot_general(stacked, keys, (((1,), (1,)), ((), ())), preferred_element_type=jnp.float32)
        scores = (scores.reshape(8, 128, 128) + bias[...][None]).reshape(1024, 128)
        top = jnp.max(scores, axis=1, keepdims=True)
        if first:
            new_top = jnp.broadcast_to(jnp.maximum(top, LOWEST), (1024, 128))
            weights = jnp.exp2((scores - new_top) * EXPONENT)
            total = weights
            weighted = jnp.dot(weights.astype(jnp.bfloat16), values, preferred_element_type=jnp.float32)
        else:
            old_top = tops[kind, group]
            new_top = jnp.maximum(old_top, top)
            weights = jnp.exp2((scores - new_top) * EXPONENT)
            factor = jnp.exp2((old_top - new_top) * EXPONENT)
            total = totals[kind, group] * factor + weights
            weighted = sums[kind, group] * factor + jnp.dot(
                weights.astype(jnp.bfloat16), values, preferred_element_type=jnp.float32
            )
        tops[kind, group] = new_top
        totals[kind, group] = total
        sums[kind, group] = weighted


def finish(staged, totals, sums, kind):
    for head in range(16):
        rows = slice((head % 8) * 128, (head % 8 + 1) * 128)
        total = jnp.sum(totals[kind, head // 8, rows, :], axis=1, keepdims=True)
        positive = total > 0.0
        inverse = jnp.where(positive, 1.0 / jnp.where(positive, total, 1.0), 0.0)
        result = sums[kind, head // 8, rows, :] * inverse
        staged[kind, :, head * HEAD_DIM : (head + 1) * HEAD_DIM] = result.astype(jnp.bfloat16)


def kernel(
    blocks,
    self_queries,
    cross_queries,
    text,
    images,
    lengths,
    image_places,
    self_out,
    cross_out,
    queries,
    chunks,
    staged,
    bias,
    begins,
    tops,
    totals,
    sums,
    local_sems,
    send_sems,
    recv_sems,
):
    block = lax.axis_index("ctx")
    lane = lax.axis_index("tp")
    place = lax.rem(block, ROW)
    core = lax.rem(lane, 2)
    other_lane = lane + 1 - 2 * core
    far_lane = lax.rem(lane + 2, 4)
    other_far_lane = lax.rem(other_lane + 2, 4)

    def at(step, to_lane):
        return (lax.rem(block + step + blocks, blocks), to_lane)

    barrier = pltpu.get_barrier_semaphore()

    def greet(step, to_lane):
        pl.semaphore_signal(barrier, inc=1, device_id=at(step, to_lane), device_id_type=MESH)

    greet(0, other_lane)

    @pl.when(place >= 1)
    def _():
        greet(-1, lane)

    @pl.when(place <= 2)
    def _():
        greet(1, lane)
        greet(-3, lane)

    @pl.when(place >= 2)
    def _():
        greet(3, lane)

    @pl.when(place == 0)
    def _():
        greet(-1, far_lane)
        greet(-2, far_lane)

    @pl.when(place == 3)
    def _():
        greet(-3, far_lane)
        greet(-2, far_lane)

    def columns(of_lane):
        return images.at[:, :, :, pl.ds(pl.multiple_of(of_lane * 256, 256), 256)]

    loads = [
        pltpu.make_async_copy(text, chunks.at[TEXT + OWN], local_sems.at[0]),
        pltpu.make_async_copy(columns(lane), chunks.at[NEAR + OWN, :, :, core], local_sems.at[1]),
        pltpu.make_async_copy(columns(far_lane), chunks.at[FAR + OWN, :, :, core], local_sems.at[2]),
        pltpu.make_async_copy(self_queries, queries.at[0], local_sems.at[3]),
        pltpu.make_async_copy(cross_queries, queries.at[1], local_sems.at[4]),
    ]
    for load in loads:
        load.start()

    row_index = lax.broadcasted_iota(jnp.int32, (64, 64), 0)
    column_index = lax.broadcasted_iota(jnp.int32, (64, 64), 1)
    spread = jnp.broadcast_to(lengths[...].astype(jnp.float32), (64, 64))
    starts = jnp.sum(jnp.where(column_index < row_index, spread, 0.0), axis=1, keepdims=True)
    starts = jnp.sum(jnp.where(column_index == row_index, starts, 0.0), axis=0, keepdims=True)
    tokens = block * 128 + lax.broadcasted_iota(jnp.int32, (128, 64), 0)
    begin = jnp.max(jnp.where(starts <= tokens.astype(jnp.float32), starts, 0.0), axis=1, keepdims=True)
    begins[...] = jnp.broadcast_to(begin, (128, 128)).astype(jnp.int32)

    def mask(positions):
        token = block * 128 + lax.broadcasted_iota(jnp.int32, (128, 128), 0)
        seen = (positions >= begins[...]) & (positions <= token)
        bias[...] = jnp.where(seen, 0.0, HIDDEN)

    def take(group, source, chunk, first):
        index = lax.broadcasted_iota(jnp.int32, (128, 128), 1)
        if group == TEXT:
            mask(source * 128 + index)
        else:
            slot = jnp.maximum(source, 0) * 2
            left = jnp.where(source >= 0, image_places[slot], -1)
            right = jnp.where(source >= 0, image_places[slot + 1], -1)
            mask(jnp.where(index < 64, left, right))
        kind = 0 if group == TEXT else 1
        attend(queries, chunks, bias, tops, totals, sums, kind, chunk, first)

    def send(source, target, sem, receive, device):
        return pltpu.make_async_remote_copy(
            src_ref=source,
            dst_ref=target,
            send_sem=send_sems.at[sem],
            recv_sem=recv_sems.at[receive],
            device_id=device,
            device_id_type=MESH,
        )

    def own(group, sem, step):
        return send(chunks.at[group + OWN], chunks.at[group + place], sem, group + place, at(step, lane))

    pl.semaphore_wait(barrier, pick(place, (3, 6, 6, 4)))
    swap_near = send(columns(other_lane), chunks.at[NEAR + OWN, :, :, core], 0, NEAR + OWN, at(0, other_lane))
    swap_far = send(columns(other_far_lane), chunks.at[FAR + OWN, :, :, core], 1, FAR + OWN, at(0, other_lane))
    swap_far.start()
    swap_near.start()

    def own_to_row(group, sem):
        ahead, across = own(group, sem, 1), own(group, sem + 1, 3)

        @pl.when(place <= 2)
        def _():
            ahead.start()

        @pl.when(place >= 1)
        def _():
            across.start()

    def own_to_row_wait(group, sem):
        ahead, across = own(group, sem, 1), own(group, sem + 1, 3)

        @pl.when(place <= 2)
        def _():
            ahead.wait_send()

        @pl.when(place >= 1)
        def _():
            across.wait_send()

    loads[0].wait()
    own_to_row(TEXT, 2)
    loads[2].wait()
    swap_far.wait_recv()
    to_far = send(
        chunks.at[FAR + OWN], chunks.at[FAR + place], 4, FAR + place, at(pick(place, FAR_STEP), far_lane)
    )
    to_far.start()
    loads[1].wait()
    swap_near.wait_recv()
    own_to_row(NEAR, 5)
    loads[3].wait()
    take(TEXT, block, TEXT + OWN, True)
    loads[4].wait()
    take(NEAR, block, NEAR + OWN, True)

    forwards = []
    self_left = 3
    store_self = pltpu.make_async_copy(staged.at[0], self_out, local_sems.at[5])
    for number, (group, sources, steps) in enumerate(ARRIVALS):
        source = pick(place, sources)
        chunk = group + source
        step = pick(place, steps)
        forward = send(chunks.at[chunk], chunks.at[chunk], 7 + number, chunk, at(step, lane))
        forward.wait_recv()

        @pl.when(step != 0)
        def _(forward=forward):
            forward.start()

        forwards.append((step, forward))
        take(group, block - place + source - jnp.where(source > place, ROW, 0), chunk, False)
        if group == TEXT:
            self_left -= 1
            if self_left == 0:
                finish(staged, totals, sums, 0)
                store_self.start()
    finish(staged, totals, sums, 1)
    store_cross = pltpu.make_async_copy(staged.at[1], cross_out, local_sems.at[6])
    store_cross.start()
    swap_near.wait_send()
    swap_far.wait_send()
    to_far.wait_send()
    own_to_row_wait(TEXT, 2)
    own_to_row_wait(NEAR, 5)
    for step, forward in forwards:

        @pl.when(step != 0)
        def _(forward=forward):
            forward.wait_send()

    store_self.wait()
    store_cross.wait()


def per_device(self_queries, cross_queries, text_pairs, image_pairs, doc_lengths, image_places):
    anywhere = pl.BlockSpec(memory_space=pl.ANY)
    result = jax.ShapeDtypeStruct(self_queries.shape, jnp.bfloat16)
    state = pltpu.VMEM((2, 2, 1024, HEAD_DIM), jnp.float32)
    return pl.pallas_call(
        functools.partial(kernel, lax.axis_size("ctx")),
        out_shape=(result, result),
        in_specs=[
            anywhere,
            anywhere,
            anywhere,
            anywhere,
            pl.BlockSpec(memory_space=pltpu.VMEM),
            pl.BlockSpec(memory_space=pltpu.SMEM),
        ],
        out_specs=(anywhere, anywhere),
        scratch_shapes=[
            pltpu.VMEM((2, 128, 2048), jnp.bfloat16),
            pltpu.VMEM((15, 2, 2, 2, 32, 256), jnp.bfloat16),
            pltpu.VMEM((2, 128, 2048), jnp.bfloat16),
            pltpu.VMEM((128, 128), jnp.float32),
            pltpu.VMEM((128, 128), jnp.int32),
            state,
            state,
            state,
            pltpu.SemaphoreType.DMA((7,)),
            pltpu.SemaphoreType.DMA((7 + len(ARRIVALS),)),
            pltpu.SemaphoreType.DMA((15,)),
        ],
        compiler_params=pltpu.CompilerParams(
            collective_id=0, has_side_effects=True, vmem_limit_bytes=40 << 20
        ),
    )(
        self_queries,
        cross_queries,
        text_pairs.reshape(2, 2, 2, 32, 256),
        image_pairs,
        doc_lengths.reshape(1, 64),
        image_places,
    )


def solution(mesh):
    placed = (
        P("ctx", "tp"),
        P("ctx", "tp"),
        P(None, "ctx", "tp"),
        P(None, "ctx", "tp", None),
        P(),
        P(),
    )
    return jax.shard_map(
        per_device,
        mesh=mesh,
        in_specs=placed,
        out_specs=(P("ctx", "tp"), P("ctx", "tp")),
        check_vma=False,
    )
```

```python
import functools
import math
import jax
import jax.numpy as jnp
from jax import lax
from jax.experimental import pallas as pl
from jax.experimental.pallas import tpu as pltpu
from jax.sharding import PartitionSpec as P

HEAD_DIM = 128
ROW = 4
OWN = 4
TEXT, NEAR, FAR = 0, 5, 10
HIDDEN = -1e30
LOWEST = -1e29
EXPONENT = math.log2(math.e) / math.sqrt(HEAD_DIM)
MESH = pl.DeviceIdType.MESH

ORDER = (
    ("G3a", "G2a", "T1a", "I1a", "T2a", "G2b", "T1b", "I1b", "T2b", "G3b", "I2b", "G0a", "I3a", "T3b", "I3b", "T3a", "I2a", "G0b", "G1a", "G1b"),
    ("T0b", "T2a", "I0b", "T0a", "I0a", "T2b", "I2a", "I2b", "T3b", "G3a", "T3a", "G2a", "I3a", "G2b", "I3b", "G3b", "G1a", "G0a", "G0b", "G1b"),
    ("T1b", "T1a", "T3b", "T3a", "I3a", "I1a", "T0b", "I3b", "G0a", "I1b", "I0a", "G1a", "I0b", "T0a", "G0b", "G1b", "G3a", "G2a", "G2b", "G3b"),
    ("G0a", "G1a", "I2a", "I2b", "G0b", "T1a", "G1b", "I0a", "T1b", "T2b", "T0a", "G3a", "G2a", "I0b", "I1b", "I1a", "T0b", "T2a", "G2b", "G3b"),
)
CLASSES = {"T": TEXT, "I": NEAR, "G": FAR}
PARTS = {"a": 0, "b": 1}
FAR_ON = ((0, -1, -1, -1), (0, 3, -1, -1), (1, -3, 1, 0), (1, 1, -3, 0))


def onward(group, source, place):
    if group == FAR:
        return FAR_ON[source][place]
    if source < place:
        return 1 if place < ROW - 1 else 0
    return -1 if place > 0 else 0


def plan():
    orders = [[(CLASSES[word[0]], int(word[1]), PARTS[word[2]]) for word in order] for order in ORDER]
    whole = []
    for order in orders:
        seen, done = set(), []
        for number, (group, source, _) in enumerate(order):
            if (group, source) in seen:
                done.append((number, group, source))
            seen.add((group, source))
        whole.append(done)
    ready = [[] for _ in orders[0]]
    for entry in zip(*whole):
        ready[max(number for number, _, _ in entry)].append(
            (tuple(group for _, group, _ in entry), tuple(source for _, _, source in entry))
        )
    for number, entry in enumerate(zip(*orders)):
        groups, sources, parts = (tuple(column) for column in zip(*entry))
        steps = tuple(onward(groups[place], sources[place], place) for place in range(ROW))
        yield groups, sources, parts, steps, ready[number]


FAR_STEP = (3, 2, 2, 1)
FAR_STEP_LAST = (3, 2, 0, 0)


def pick(place, values):
    result = jnp.int32(values[-1])
    for index, value in enumerate(values[:-1]):
        result = jnp.where(place == index, value, result)
    return result


def attend(queries, chunks, bias, tops, totals, sums, kind, chunk, first):
    for group in range(2):
        columns = slice(group * HEAD_DIM, (group + 1) * HEAD_DIM)
        keys = chunks[chunk, 0, :, :, :, columns].reshape(HEAD_DIM, HEAD_DIM)
        values = chunks[chunk, 1, :, :, :, columns].reshape(HEAD_DIM, HEAD_DIM)
        heads = [queries[kind, :, h * HEAD_DIM : (h + 1) * HEAD_DIM] for h in range(group * 8, group * 8 + 8)]
        stacked = jnp.concatenate(heads, axis=0)
        scores = lax.dot_general(stacked, keys, (((1,), (1,)), ((), ())), preferred_element_type=jnp.float32)
        scores = (scores.reshape(8, 128, 128) + bias[...][None]).reshape(1024, 128)
        top = jnp.max(scores, axis=1, keepdims=True)
        if first:
            new_top = jnp.broadcast_to(jnp.maximum(top, LOWEST), (1024, 128))
            weights = jnp.exp2((scores - new_top) * EXPONENT)
            total = weights
            weighted = jnp.dot(weights.astype(jnp.bfloat16), values, preferred_element_type=jnp.float32)
        else:
            old_top = tops[kind, group]
            new_top = jnp.maximum(old_top, top)
            weights = jnp.exp2((scores - new_top) * EXPONENT)
            factor = jnp.exp2((old_top - new_top) * EXPONENT)
            total = totals[kind, group] * factor + weights
            weighted = sums[kind, group] * factor + jnp.dot(
                weights.astype(jnp.bfloat16), values, preferred_element_type=jnp.float32
            )
        tops[kind, group] = new_top
        totals[kind, group] = total
        sums[kind, group] = weighted


def finish(staged, totals, sums, kind):
    for head in range(16):
        rows = slice((head % 8) * 128, (head % 8 + 1) * 128)
        total = jnp.sum(totals[kind, head // 8, rows, :], axis=1, keepdims=True)
        positive = total > 0.0
        inverse = jnp.where(positive, 1.0 / jnp.where(positive, total, 1.0), 0.0)
        result = sums[kind, head // 8, rows, :] * inverse
        staged[kind, :, head * HEAD_DIM : (head + 1) * HEAD_DIM] = result.astype(jnp.bfloat16)


def kernel(
    blocks,
    self_queries,
    cross_queries,
    text,
    images,
    lengths_hbm,
    places_hbm,
    self_out,
    cross_out,
    lengths,
    image_places,
    queries,
    chunks,
    staged,
    bias,
    begins,
    tops,
    totals,
    sums,
    local_sems,
    send_sems,
    recv_sems,
):
    block = lax.axis_index("ctx")
    lane = lax.axis_index("tp")
    place = lax.rem(block, ROW)
    core = lax.rem(lane, 2)
    other_lane = lane + 1 - 2 * core
    far_lane = lax.rem(lane + 2, 4)
    other_far_lane = lax.rem(other_lane + 2, 4)

    def at(step, to_lane):
        return (lax.rem(block + step + blocks, blocks), to_lane)

    first_row = block < ROW
    last_row = block >= blocks - ROW

    barrier = pltpu.get_barrier_semaphore()

    def greet(step, to_lane):
        pl.semaphore_signal(barrier, inc=1, device_id=at(step, to_lane), device_id_type=MESH)

    greet(0, other_lane)

    @pl.when(place >= 1)
    def _():
        greet(-1, lane)

    @pl.when(place <= 2)
    def _():
        greet(1, lane)

    @pl.when((place <= 2) & ~first_row)
    def _():
        greet(-3, lane)

    @pl.when((place >= 2) & ~last_row)
    def _():
        greet(3, lane)

    @pl.when((place >= 2) & last_row)
    def _():
        greet(0, far_lane)

    @pl.when((place == 0) & ~first_row)
    def _():
        greet(-1, far_lane)
        greet(-2, far_lane)

    @pl.when(place == 3)
    def _():
        greet(-3, far_lane)
        greet(-2, far_lane)

    def columns(of_lane):
        return images.at[:, :, :, pl.ds(pl.multiple_of(of_lane * 256, 256), 256)]

    loads = [
        pltpu.make_async_copy(text, chunks.at[TEXT + OWN], local_sems.at[0]),
        pltpu.make_async_copy(columns(lane), chunks.at[NEAR + OWN, :, :, core], local_sems.at[1]),
        pltpu.make_async_copy(columns(far_lane), chunks.at[FAR + OWN, :, :, core], local_sems.at[2]),
        pltpu.make_async_copy(self_queries, queries.at[0], local_sems.at[3]),
        pltpu.make_async_copy(cross_queries, queries.at[1], local_sems.at[4]),
        pltpu.make_async_copy(lengths_hbm, lengths, local_sems.at[7]),
        pltpu.make_async_copy(places_hbm, image_places, local_sems.at[8]),
    ]
    for load in loads:
        load.start()

    loads[5].wait()
    loads[6].wait()

    row_index = lax.broadcasted_iota(jnp.int32, (64, 64), 0)
    column_index = lax.broadcasted_iota(jnp.int32, (64, 64), 1)
    spread = jnp.broadcast_to(lengths[...].astype(jnp.float32), (64, 64))
    starts = jnp.sum(jnp.where(column_index < row_index, spread, 0.0), axis=1, keepdims=True)
    starts = jnp.sum(jnp.where(column_index == row_index, starts, 0.0), axis=0, keepdims=True)
    tokens = block * 128 + lax.broadcasted_iota(jnp.int32, (128, 64), 0)
    begin = jnp.max(jnp.where(starts <= tokens.astype(jnp.float32), starts, 0.0), axis=1, keepdims=True)
    begins[...] = jnp.broadcast_to(begin, (128, 128)).astype(jnp.int32)

    def mask(positions):
        token = block * 128 + lax.broadcasted_iota(jnp.int32, (128, 128), 0)
        seen = (positions >= begins[...]) & (positions <= token)
        bias[...] = jnp.where(seen, 0.0, HIDDEN)

    def take(group, source, chunk, first):
        index = lax.broadcasted_iota(jnp.int32, (128, 128), 1)
        slot = jnp.maximum(source, 0) * 2
        left = jnp.where(source >= 0, image_places[slot], -1)
        right = jnp.where(source >= 0, image_places[slot + 1], -1)
        mask(jnp.where(group == TEXT, source * 128 + index, jnp.where(index < 64, left, right)))
        kind = jnp.where(group == TEXT, 0, 1)
        attend(queries, chunks, bias, tops, totals, sums, kind, chunk, first)

    def send(source, target, sem, receive, device):
        return pltpu.make_async_remote_copy(
            src_ref=source,
            dst_ref=target,
            send_sem=send_sems.at[sem],
            recv_sem=receive,
            device_id=device,
            device_id_type=MESH,
        )

    def sources_of_own(group, sem):
        for part in range(2):
            for kind, (step, goes) in enumerate(((1, place <= 2), (3, (place >= 1) & ~last_row))):
                yield goes, send(
                    chunks.at[group + OWN, part],
                    chunks.at[group + place, part],
                    sem + 2 * part + kind,
                    recv_sems.at[group + place, part],
                    at(step, lane),
                )

    expected = pick(place, (3, 6, 6, 4)) - jnp.where(last_row & (place >= 1), 1, 0)
    expected = expected - jnp.where(first_row & ((place == 1) | (place == 2)), 1, 0)
    pl.semaphore_wait(barrier, expected)
    own_near, own_far = NEAR + OWN, FAR + OWN
    swap_far = send(
        columns(other_far_lane), chunks.at[own_far, :, :, core], 0, recv_sems.at[own_far, 0], at(0, other_lane)
    )
    swap_near = send(
        columns(other_lane), chunks.at[own_near, :, :, core], 1, recv_sems.at[own_near, 0], at(0, other_lane)
    )
    swap_far.start()
    swap_near.start()

    def start(copies):
        for goes, copy in copies:

            @pl.when(goes)
            def _(copy=copy):
                copy.start()

    loads[0].wait()
    sent = list(sources_of_own(TEXT, 2))
    start(sent)
    loads[2].wait()
    swap_far.wait_recv()
    far_step = jnp.where(last_row, pick(place, FAR_STEP_LAST), pick(place, FAR_STEP))
    to_far = [
        send(
            chunks.at[own_far, part],
            chunks.at[FAR + place, part],
            6 + part,
            recv_sems.at[FAR + place, part],
            at(far_step, far_lane),
        )
        for part in range(2)
    ]
    for copy in to_far:
        copy.start()
    loads[1].wait()
    swap_near.wait_recv()
    sent_near = list(sources_of_own(NEAR, 8))
    start(sent_near)
    sent += sent_near
    loads[3].wait()
    take(TEXT, block, TEXT + OWN, True)
    loads[4].wait()
    take(NEAR, block, NEAR + OWN, True)

    store_self = pltpu.make_async_copy(staged.at[0], self_out, local_sems.at[5])
    for number, (groups, sources, parts, steps, ready) in enumerate(plan()):
        group, source, part, step = (pick(place, table) for table in (groups, sources, parts, steps))
        chunk = group + source
        origin = block - place + source - jnp.where(source > place, ROW, 0)
        forward = send(
            chunks.at[chunk, part], chunks.at[chunk, part], 12 + number, recv_sems.at[chunk, part], at(step, lane)
        )
        goes = (origin >= 0) & (step != 0) & ~((step == 3) & last_row)
        if number == len(ORDER[0]) - 1:
            finish(staged, totals, sums, 0)
            store_self.start()

        @pl.when(origin >= 0)
        def _(forward=forward):
            forward.wait_recv()

        @pl.when(goes)
        def _(forward=forward):
            forward.start()

        sent.append((goes, forward))
        for whole_groups, whole_sources in ready:
            group, source = pick(place, whole_groups), pick(place, whole_sources)
            origin = block - place + source - jnp.where(source > place, ROW, 0)

            @pl.when(origin >= 0)
            def _(group=group, source=source, origin=origin):
                take(group, origin, group + source, False)

    finish(staged, totals, sums, 1)
    store_cross = pltpu.make_async_copy(staged.at[1], cross_out, local_sems.at[6])
    store_cross.start()
    swap_near.wait_send()
    swap_far.wait_send()
    for copy in to_far:
        copy.wait_send()
    for goes, copy in sent:

        @pl.when(goes)
        def _(copy=copy):
            copy.wait_send()

    store_self.wait()
    store_cross.wait()


def per_device(self_queries, cross_queries, text_pairs, image_pairs, doc_lengths, image_places):
    anywhere = pl.BlockSpec(memory_space=pl.ANY)
    result = jax.ShapeDtypeStruct(self_queries.shape, jnp.bfloat16)
    state = pltpu.VMEM((2, 2, 1024, HEAD_DIM), jnp.float32)
    return pl.pallas_call(
        functools.partial(kernel, lax.axis_size("ctx")),
        out_shape=(result, result),
        in_specs=[anywhere] * 6,
        out_specs=(anywhere, anywhere),
        scratch_shapes=[
            pltpu.VMEM((1, 64), jnp.int32),
            pltpu.SMEM((256,), jnp.int32),
            pltpu.VMEM((2, 128, 2048), jnp.bfloat16),
            pltpu.VMEM((15, 2, 2, 2, 32, 256), jnp.bfloat16),
            pltpu.VMEM((2, 128, 2048), jnp.bfloat16),
            pltpu.VMEM((128, 128), jnp.float32),
            pltpu.VMEM((128, 128), jnp.int32),
            state,
            state,
            state,
            pltpu.SemaphoreType.DMA((9,)),
            pltpu.SemaphoreType.DMA((12 + len(ORDER[0]),)),
            pltpu.SemaphoreType.DMA((15, 2)),
        ],
        compiler_params=pltpu.CompilerParams(
            collective_id=0, has_side_effects=True, vmem_limit_bytes=60 << 20
        ),
    )(
        self_queries,
        cross_queries,
        text_pairs.reshape(2, 2, 2, 32, 256),
        image_pairs,
        doc_lengths.reshape(1, 64),
        image_places,
    )


def solution(mesh):
    placed = (
        P("ctx", "tp"),
        P("ctx", "tp"),
        P(None, "ctx", "tp"),
        P(None, "ctx", "tp", None),
        P(),
        P(),
    )
    return jax.shard_map(
        per_device,
        mesh=mesh,
        in_specs=placed,
        out_specs=(P("ctx", "tp"), P("ctx", "tp")),
        check_vma=False,
    )
```

```python
import functools
import math
import jax
import jax.numpy as jnp
from jax import lax
from jax.experimental import pallas as pl
from jax.experimental.pallas import tpu as pltpu
from jax.sharding import PartitionSpec as P

HEAD_DIM = 128
ROW = 4
OWN = 4
TEXT, NEAR, FAR = 0, 5, 10
HIDDEN = -1e30
LOWEST = -1e29
EXPONENT = math.log2(math.e) / math.sqrt(HEAD_DIM)
MESH = pl.DeviceIdType.MESH

ORDER = (
    ("G3a", "T1a", "G2a", "I1a", "T2a", "G3b", "T2b", "G2b", "T1b", "I3a", "G0a", "T3a", "I2a", "I1b", "T3b", "I3b", "G0b", "G1b", "I2b", "G1a"),
    ("T0b", "T0a", "T2b", "I0a", "T2a", "I2a", "I2b", "I0b", "T3b", "G3a", "T3a", "I3a", "G2a", "I3b", "G3b", "G0a", "G1b", "G2b", "G0b", "G1a"),
    ("T1a", "T3b", "T1b", "I1b", "T3a", "I3a", "T0b", "I3b", "I1a", "T0a", "G0a", "G1b", "I0b", "I0a", "G0b", "G3a", "G1a", "G2a", "G3b", "G2b"),
    ("G0a", "G1b", "G1a", "T1a", "T2a", "G0b", "I1a", "I0b", "I0a", "T2b", "T0b", "T0a", "I2a", "G2a", "T1b", "I2b", "G3b", "G3a", "I1b", "G2b"),
)
CLASSES = {"T": TEXT, "I": NEAR, "G": FAR}
PARTS = {"a": 0, "b": 1}
FAR_ON = ((0, -1, -1, -1), (0, 3, -1, -1), (1, -3, 1, 0), (1, 1, -3, 0))


def onward(group, source, place):
    if group == FAR:
        return FAR_ON[source][place]
    if source < place:
        return 1 if place < ROW - 1 else 0
    return -1 if place > 0 else 0


def plan():
    orders = [[(CLASSES[word[0]], int(word[1]), PARTS[word[2]]) for word in order] for order in ORDER]
    whole = []
    for order in orders:
        seen, done = set(), []
        for number, (group, source, _) in enumerate(order):
            if (group, source) in seen:
                done.append((number, group, source))
            seen.add((group, source))
        whole.append(done)
    ready = [[] for _ in orders[0]]
    for entry in zip(*whole):
        ready[max(number for number, _, _ in entry)].append(
            (tuple(group for _, group, _ in entry), tuple(source for _, _, source in entry))
        )
    for number, entry in enumerate(zip(*orders)):
        groups, sources, parts = (tuple(column) for column in zip(*entry))
        steps = tuple(onward(groups[place], sources[place], place) for place in range(ROW))
        yield groups, sources, parts, steps, ready[number]


FAR_STEP = (3, 2, 2, 1)
FAR_STEP_LAST = (3, 2, 0, 0)


def pick(place, values):
    result = jnp.int32(values[-1])
    for index, value in enumerate(values[:-1]):
        result = jnp.where(place == index, value, result)
    return result


def normalized(weighted, totals):
    total = jnp.sum(totals, axis=1, keepdims=True)
    positive = total > 0.0
    inverse = jnp.where(positive, 1.0 / jnp.where(positive, total, 1.0), 0.0)
    return (weighted * inverse).astype(jnp.bfloat16)


def attend(queries, chunks, bias, tops, totals, sums, kind, chunk, first, results=None):
    for group in range(2):
        columns = slice(group * HEAD_DIM, (group + 1) * HEAD_DIM)
        keys = chunks[chunk, 0, :, :, :, columns].reshape(HEAD_DIM, HEAD_DIM)
        values = chunks[chunk, 1, :, :, :, columns].reshape(HEAD_DIM, HEAD_DIM)
        heads = [queries[kind, :, h * HEAD_DIM : (h + 1) * HEAD_DIM] for h in range(group * 8, group * 8 + 8)]
        stacked = jnp.concatenate(heads, axis=0)
        scores = lax.dot_general(stacked, keys, (((1,), (1,)), ((), ())), preferred_element_type=jnp.float32)
        scores = (scores.reshape(8, 128, 128) + bias[...][None]).reshape(1024, 128)
        top = jnp.max(scores, axis=1, keepdims=True)
        if first:
            new_top = jnp.broadcast_to(jnp.maximum(top, LOWEST), (1024, 128))
            weights = jnp.exp2((scores - new_top) * EXPONENT)
            total = weights
            weighted = jnp.dot(weights.astype(jnp.bfloat16), values, preferred_element_type=jnp.float32)
        else:
            old_top = tops[kind, group]
            new_top = jnp.maximum(old_top, top)
            weights = jnp.exp2((scores - new_top) * EXPONENT)
            factor = jnp.exp2((old_top - new_top) * EXPONENT)
            total = totals[kind, group] * factor + weights
            weighted = sums[kind, group] * factor + jnp.dot(
                weights.astype(jnp.bfloat16), values, preferred_element_type=jnp.float32
            )
        if results is not None:
            scaled = normalized(weighted, total)
            for head in range(8):
                columns = slice((group * 8 + head) * HEAD_DIM, (group * 8 + head + 1) * HEAD_DIM)
                results[1, :, columns] = scaled[head * 128 : (head + 1) * 128]
            continue
        tops[kind, group] = new_top
        totals[kind, group] = total
        sums[kind, group] = weighted


def finish(results, totals, sums, kind):
    for head in range(16):
        rows = slice((head % 8) * 128, (head % 8 + 1) * 128)
        scaled = normalized(sums[kind, head // 8, rows, :], totals[kind, head // 8, rows, :])
        results[kind, :, head * HEAD_DIM : (head + 1) * HEAD_DIM] = scaled


def kernel(
    blocks,
    self_queries,
    cross_queries,
    text,
    images,
    lengths_hbm,
    places_hbm,
    results,
    lengths,
    image_places,
    queries,
    chunks,
    bias,
    begins,
    tops,
    totals,
    sums,
    local_sems,
    send_sems,
    recv_sems,
    far_ready,
):
    block = lax.axis_index("ctx")
    lane = lax.axis_index("tp")
    place = lax.rem(block, ROW)
    core = lax.rem(lane, 2)
    other_lane = lane + 1 - 2 * core
    far_lane = lax.rem(lane + 2, 4)
    other_far_lane = lax.rem(other_lane + 2, 4)

    def at(step, to_lane):
        return (lax.rem(block + step + blocks, blocks), to_lane)

    half = lane // 2
    first_row = block < ROW
    last_row = block >= blocks - ROW

    barrier = pltpu.get_barrier_semaphore()

    def greet(step, to_lane):
        pl.semaphore_signal(barrier, inc=1, device_id=at(step, to_lane), device_id_type=MESH)

    greet(0, other_lane)

    @pl.when(place >= 1)
    def _():
        greet(-1, lane)

    @pl.when(place <= 2)
    def _():
        greet(1, lane)

    @pl.when((place <= 2) & ~first_row)
    def _():
        greet(-3, lane)

    @pl.when((place >= 2) & ~last_row)
    def _():
        greet(3, lane)

    far_step = jnp.where(last_row, pick(place, FAR_STEP_LAST), pick(place, FAR_STEP))

    @pl.when(half == 0)
    def _():
        greet(far_step, far_lane)

    def for_far_sources(tell):
        @pl.when((place >= 2) & last_row)
        def _():
            tell(0, far_lane)

        @pl.when((place == 0) & ~first_row)
        def _():
            tell(-1, far_lane)
            tell(-2, far_lane)

        @pl.when(place == 3)
        def _():
            tell(-3, far_lane)
            tell(-2, far_lane)

    @pl.when(half == 0)
    def _():
        for_far_sources(greet)

    def columns(of_lane):
        return images.at[:, :, :, pl.ds(pl.multiple_of(of_lane * 256, 256), 256)]

    loads = [
        pltpu.make_async_copy(text, chunks.at[TEXT + OWN], local_sems.at[0]),
        pltpu.make_async_copy(columns(lane), chunks.at[NEAR + OWN, :, :, core], local_sems.at[1]),
        pltpu.make_async_copy(columns(far_lane), chunks.at[FAR + OWN, :, :, core], local_sems.at[2]),
        pltpu.make_async_copy(self_queries, queries.at[0], local_sems.at[3]),
        pltpu.make_async_copy(cross_queries, queries.at[1], local_sems.at[4]),
        pltpu.make_async_copy(lengths_hbm, lengths, local_sems.at[5]),
        pltpu.make_async_copy(places_hbm, image_places, local_sems.at[6]),
    ]
    for load in loads:
        load.start()

    loads[5].wait()
    loads[6].wait()

    row_index = lax.broadcasted_iota(jnp.int32, (64, 64), 0)
    column_index = lax.broadcasted_iota(jnp.int32, (64, 64), 1)
    spread = jnp.broadcast_to(lengths[...].astype(jnp.float32), (64, 64))
    starts = jnp.sum(jnp.where(column_index < row_index, spread, 0.0), axis=1, keepdims=True)
    starts = jnp.sum(jnp.where(column_index == row_index, starts, 0.0), axis=0, keepdims=True)
    tokens = block * 128 + lax.broadcasted_iota(jnp.int32, (128, 64), 0)
    begin = jnp.max(jnp.where(starts <= tokens.astype(jnp.float32), starts, 0.0), axis=1, keepdims=True)
    begins[...] = jnp.broadcast_to(begin, (128, 128)).astype(jnp.int32)

    def mask(positions):
        token = block * 128 + lax.broadcasted_iota(jnp.int32, (128, 128), 0)
        seen = (positions >= begins[...]) & (positions <= token)
        bias[...] = jnp.where(seen, 0.0, HIDDEN)

    def take(group, source, chunk, first, last_results=None):
        index = lax.broadcasted_iota(jnp.int32, (128, 128), 1)
        slot = jnp.maximum(source, 0) * 2
        left = jnp.where(source >= 0, image_places[slot], -1)
        right = jnp.where(source >= 0, image_places[slot + 1], -1)
        mask(jnp.where(group == TEXT, source * 128 + index, jnp.where(index < 64, left, right)))
        kind = jnp.where(group == TEXT, 0, 1)
        attend(queries, chunks, bias, tops, totals, sums, kind, chunk, first, last_results)

    def send(source, target, sem, receive, device):
        return pltpu.make_async_remote_copy(
            src_ref=source,
            dst_ref=target,
            send_sem=send_sems.at[sem],
            recv_sem=receive,
            device_id=device,
            device_id_type=MESH,
        )

    def sources_of_own(group, sem):
        for part in range(2):
            for kind, (step, goes) in enumerate(((1, place <= 2), (3, (place >= 1) & ~last_row))):
                yield goes, send(
                    chunks.at[group + OWN, part],
                    chunks.at[group + place, part],
                    sem + 2 * part + kind,
                    recv_sems.at[group + place, part],
                    at(step, lane),
                )

    expected = pick(place, (3, 6, 6, 4)) - jnp.where(last_row & (place >= 1), 1, 0)
    expected = expected - jnp.where(first_row & ((place == 1) | (place == 2)), 1, 0)
    far_sources = pick(place, (2, 0, 0, 2)) - jnp.where(first_row & (place == 0), 2, 0)
    far_sources = far_sources + jnp.where(last_row & (place >= 2), 1, 0)
    pl.semaphore_wait(barrier, expected + jnp.where(half == 0, -1, far_sources))

    def invite(step, to_lane):
        pl.semaphore_signal(far_ready, inc=1, device_id=at(step, to_lane), device_id_type=MESH)

    @pl.when(half == 1)
    def _():
        for_far_sources(invite)

    own_near, own_far = NEAR + OWN, FAR + OWN
    swap_far = send(
        columns(other_far_lane), chunks.at[own_far, :, :, core], 0, recv_sems.at[own_far, 0], at(0, other_lane)
    )
    swap_near = send(
        columns(other_lane), chunks.at[own_near, :, :, core], 1, recv_sems.at[own_near, 0], at(0, other_lane)
    )
    swap_far.start()
    swap_near.start()

    def start(copies):
        for goes, copy in copies:

            @pl.when(goes)
            def _(copy=copy):
                copy.start()

    loads[0].wait()
    sent = list(sources_of_own(TEXT, 2))
    start(sent)
    loads[2].wait()
    swap_far.wait_recv()
    to_far = [
        send(
            chunks.at[own_far, part],
            chunks.at[FAR + place, part],
            6 + part,
            recv_sems.at[FAR + place, part],
            at(far_step, far_lane),
        )
        for part in range(2)
    ]
    @pl.when(half == 1)
    def _():
        for copy in to_far:
            copy.start()

    loads[1].wait()
    swap_near.wait_recv()
    sent_near = list(sources_of_own(NEAR, 8))
    start(sent_near)

    sent += sent_near
    loads[3].wait()
    take(TEXT, block, TEXT + OWN, True)

    @pl.when(half == 0)
    def _():
        pl.semaphore_wait(far_ready, 1)
        for copy in to_far:
            copy.start()

    loads[4].wait()
    take(NEAR, block, NEAR + OWN, True)

    taken, text_left, finished = 0, [ROW - 1] * ROW, False
    for number, (groups, sources, parts, steps, ready) in enumerate(plan()):
        group, source, part, step = (pick(place, table) for table in (groups, sources, parts, steps))
        chunk = group + source
        origin = block - place + source - jnp.where(source > place, ROW, 0)
        forward = send(
            chunks.at[chunk, part], chunks.at[chunk, part], 12 + number, recv_sems.at[chunk, part], at(step, lane)
        )
        goes = (origin >= 0) & (step != 0) & ~((step == 3) & last_row)
        @pl.when(origin >= 0)
        def _(forward=forward):
            forward.wait_recv()

        @pl.when(goes)
        def _(forward=forward):
            forward.start()

        sent.append((goes, forward))
        for whole_groups, whole_sources in ready:
            group, source = pick(place, whole_groups), pick(place, whole_sources)
            origin = block - place + source - jnp.where(source > place, ROW, 0)
            taken += 1
            last_results = results if taken == 10 else None

            @pl.when(origin >= 0)
            def _(group=group, source=source, origin=origin, last_results=last_results):
                take(group, origin, group + source, False, last_results)

            if last_results is not None:

                @pl.when(origin < 0)
                def _():
                    finish(results, totals, sums, 1)

            text_left = [left - (at_place == TEXT) for left, at_place in zip(text_left, whole_groups)]
            if not finished and max(text_left) == 0:
                finished = True
                finish(results, totals, sums, 0)

    swap_near.wait_send()
    swap_far.wait_send()
    for copy in to_far:
        copy.wait_send()
    for goes, copy in sent:

        @pl.when(goes)
        def _(copy=copy):
            copy.wait_send()


def per_device(self_queries, cross_queries, text_pairs, image_pairs, doc_lengths, image_places):
    anywhere = pl.BlockSpec(memory_space=pl.ANY)
    state = pltpu.VMEM((2, 2, 1024, HEAD_DIM), jnp.float32)
    results = pl.pallas_call(
        functools.partial(kernel, lax.axis_size("ctx")),
        out_shape=pltpu.VMEM((2, *self_queries.shape), jnp.bfloat16),
        in_specs=[anywhere] * 6,
        out_specs=pl.BlockSpec(memory_space=pltpu.VMEM),
        scratch_shapes=[
            pltpu.VMEM((1, 64), jnp.int32),
            pltpu.SMEM((256,), jnp.int32),
            pltpu.VMEM((2, 128, 2048), jnp.bfloat16),
            pltpu.VMEM((15, 2, 2, 2, 32, 256), jnp.bfloat16),
            pltpu.VMEM((128, 128), jnp.float32),
            pltpu.VMEM((128, 128), jnp.int32),
            state,
            state,
            state,
            pltpu.SemaphoreType.DMA((7,)),
            pltpu.SemaphoreType.DMA((12 + len(ORDER[0]),)),
            pltpu.SemaphoreType.DMA((15, 2)),
            pltpu.SemaphoreType.REGULAR,
        ],
        compiler_params=pltpu.CompilerParams(
            collective_id=0, has_side_effects=True, vmem_limit_bytes=60 << 20
        ),
    )(
        self_queries,
        cross_queries,
        text_pairs.reshape(2, 2, 2, 32, 256),
        image_pairs,
        doc_lengths.reshape(1, 64),
        image_places,
    )
    return results[0], results[1]


def solution(mesh):
    placed = (
        P("ctx", "tp"),
        P("ctx", "tp"),
        P(None, "ctx", "tp"),
        P(None, "ctx", "tp", None),
        P(),
        P(),
    )
    return jax.shard_map(
        per_device,
        mesh=mesh,
        in_specs=placed,
        out_specs=(P("ctx", "tp"), P("ctx", "tp")),
        check_vma=False,
    )
```

```python
import functools
import math
import jax
import jax.numpy as jnp
from jax import lax
from jax.experimental import pallas as pl
from jax.experimental.pallas import tpu as pltpu
from jax.sharding import PartitionSpec as P

HEAD_DIM = 128
ROW = 4
OWN = 4
TEXT, NEAR, FAR = 0, 5, 10
HIDDEN = -1e30
LOWEST = -1e29
EXPONENT = math.log2(math.e) / math.sqrt(HEAD_DIM)
MESH = pl.DeviceIdType.MESH

ORDER = (
    ("G3a", "G2a", "T2b", "G2b", "T1b", "I1a", "T1a", "G3b", "I2b", "I3a", "I1b", "T3b", "I3b", "T2a", "T3a", "I2a", "G0a", "G1b", "G1a", "G0b"),
    ("T0b", "T2a", "I0a", "I0b", "T2b", "I2a", "T0a", "T3b", "I2b", "G3a", "T3a", "I3a", "G2a", "I3b", "G2b", "G1b", "G3b", "G0a", "G1a", "G0b"),
    ("T1a", "T3b", "I1a", "T3a", "I3a", "I3b", "T1b", "T0b", "I0a", "I1b", "G1b", "T0a", "G0a", "I0b", "G1a", "G3a", "G0b", "G2a", "G2b", "G3b"),
    ("G0a", "G1b", "I2a", "I1a", "G1a", "G0b", "T0a", "I0a", "I2b", "I0b", "T0b", "T1a", "T1b", "G3a", "T2b", "I1b", "G2b", "T2a", "G2a", "G3b"),
)
CLASSES = {"T": TEXT, "I": NEAR, "G": FAR}
PARTS = {"a": 0, "b": 1}
FAR_ON = ((0, -1, -1, -1), (0, 3, -1, -1), (1, -3, 1, 0), (1, 1, -3, 0))


def onward(group, source, place):
    if group == FAR:
        return FAR_ON[source][place]
    if source < place:
        return 1 if place < ROW - 1 else 0
    return -1 if place > 0 else 0


def plan():
    orders = [[(CLASSES[word[0]], int(word[1]), PARTS[word[2]]) for word in order] for order in ORDER]
    whole = []
    for order in orders:
        seen, done = set(), []
        for number, (group, source, _) in enumerate(order):
            if (group, source) in seen:
                done.append((number, group, source))
            seen.add((group, source))
        whole.append(done)
    ready = [[] for _ in orders[0]]
    for entry in zip(*whole):
        ready[max(number for number, _, _ in entry)].append(
            (tuple(group for _, group, _ in entry), tuple(source for _, _, source in entry))
        )
    for number, entry in enumerate(zip(*orders)):
        groups, sources, parts = (tuple(column) for column in zip(*entry))
        steps = tuple(onward(groups[place], sources[place], place) for place in range(ROW))
        yield groups, sources, parts, steps, ready[number]


FAR_STEP = (3, 2, 2, 1)
FAR_STEP_LAST = (3, 2, 0, 0)


def pick(place, values):
    result = jnp.int32(values[-1])
    for index, value in enumerate(values[:-1]):
        result = jnp.where(place == index, value, result)
    return result


def normalized(weighted, totals):
    total = jnp.sum(totals, axis=1, keepdims=True)
    positive = total > 0.0
    inverse = jnp.where(positive, 1.0 / jnp.where(positive, total, 1.0), 0.0)
    return (weighted * inverse).astype(jnp.bfloat16)


def attend(queries, chunks, bias, tops, totals, sums, kind, chunk, first, results=None):
    for group in range(2):
        columns = slice(group * HEAD_DIM, (group + 1) * HEAD_DIM)
        keys = chunks[chunk, 0, :, :, :, columns].reshape(HEAD_DIM, HEAD_DIM)
        values = chunks[chunk, 1, :, :, :, columns].reshape(HEAD_DIM, HEAD_DIM)
        heads = [queries[kind, :, h * HEAD_DIM : (h + 1) * HEAD_DIM] for h in range(group * 8, group * 8 + 8)]
        stacked = jnp.concatenate(heads, axis=0)
        scores = lax.dot_general(stacked, keys, (((1,), (1,)), ((), ())), preferred_element_type=jnp.float32)
        scores = (scores.reshape(8, 128, 128) + bias[...][None]).reshape(1024, 128)
        top = jnp.max(scores, axis=1, keepdims=True)
        if first:
            new_top = jnp.broadcast_to(jnp.maximum(top, LOWEST), (1024, 128))
            weights = jnp.exp2((scores - new_top) * EXPONENT)
            total = weights
            weighted = jnp.dot(weights.astype(jnp.bfloat16), values, preferred_element_type=jnp.float32)
        else:
            old_top = tops[kind, group]
            new_top = jnp.maximum(old_top, top)
            weights = jnp.exp2((scores - new_top) * EXPONENT)
            factor = jnp.exp2((old_top - new_top) * EXPONENT)
            total = totals[kind, group] * factor + weights
            weighted = sums[kind, group] * factor + jnp.dot(
                weights.astype(jnp.bfloat16), values, preferred_element_type=jnp.float32
            )
        if results is not None:
            scaled = normalized(weighted, total)
            for head in range(8):
                columns = slice((group * 8 + head) * HEAD_DIM, (group * 8 + head + 1) * HEAD_DIM)
                results[1, :, columns] = scaled[head * 128 : (head + 1) * 128]
            continue
        tops[kind, group] = new_top
        totals[kind, group] = total
        sums[kind, group] = weighted


def finish(results, totals, sums, kind):
    for head in range(16):
        rows = slice((head % 8) * 128, (head % 8 + 1) * 128)
        scaled = normalized(sums[kind, head // 8, rows, :], totals[kind, head // 8, rows, :])
        results[kind, :, head * HEAD_DIM : (head + 1) * HEAD_DIM] = scaled


def kernel(
    blocks,
    self_queries,
    cross_queries,
    text,
    images,
    lengths_hbm,
    places_hbm,
    results,
    lengths,
    image_places,
    queries,
    chunks,
    bias,
    begins,
    tops,
    totals,
    sums,
    local_sems,
    send_sems,
    recv_sems,
    far_ready,
):
    block = lax.axis_index("ctx")
    lane = lax.axis_index("tp")
    place = lax.rem(block, ROW)
    core = lax.rem(lane, 2)
    other_lane = lane + 1 - 2 * core
    far_lane = lax.rem(lane + 2, 4)
    other_far_lane = lax.rem(other_lane + 2, 4)

    def at(step, to_lane):
        return (lax.rem(block + step + blocks, blocks), to_lane)

    half = lane // 2
    first_row = block < ROW
    last_row = block >= blocks - ROW

    barrier = pltpu.get_barrier_semaphore()

    def greet(step, to_lane):
        pl.semaphore_signal(barrier, inc=1, device_id=at(step, to_lane), device_id_type=MESH)

    greet(0, other_lane)

    @pl.when(place >= 1)
    def _():
        greet(-1, lane)

    @pl.when(place <= 2)
    def _():
        greet(1, lane)

    @pl.when((place <= 2) & ~first_row)
    def _():
        greet(-3, lane)

    @pl.when((place >= 2) & ~last_row)
    def _():
        greet(3, lane)

    far_step = jnp.where(last_row, pick(place, FAR_STEP_LAST), pick(place, FAR_STEP))

    @pl.when(half == 0)
    def _():
        greet(far_step, far_lane)

    def for_far_sources(tell):
        @pl.when((place >= 2) & last_row)
        def _():
            tell(0, far_lane)

        @pl.when((place == 0) & ~first_row)
        def _():
            tell(-1, far_lane)
            tell(-2, far_lane)

        @pl.when(place == 3)
        def _():
            tell(-3, far_lane)
            tell(-2, far_lane)

    @pl.when(half == 0)
    def _():
        for_far_sources(greet)

    def columns(of_lane):
        return images.at[:, :, :, pl.ds(pl.multiple_of(of_lane * 256, 256), 256)]

    loads = [
        pltpu.make_async_copy(text, chunks.at[TEXT + OWN], local_sems.at[0]),
        pltpu.make_async_copy(columns(lane), chunks.at[NEAR + OWN, :, :, core], local_sems.at[1]),
        pltpu.make_async_copy(columns(far_lane), chunks.at[FAR + OWN, :, :, core], local_sems.at[2]),
        pltpu.make_async_copy(self_queries, queries.at[0], local_sems.at[3]),
        pltpu.make_async_copy(cross_queries, queries.at[1], local_sems.at[4]),
        pltpu.make_async_copy(lengths_hbm, lengths, local_sems.at[5]),
        pltpu.make_async_copy(places_hbm, image_places, local_sems.at[6]),
    ]
    for load in loads:
        load.start()

    loads[5].wait()
    loads[6].wait()

    row_index = lax.broadcasted_iota(jnp.int32, (64, 64), 0)
    column_index = lax.broadcasted_iota(jnp.int32, (64, 64), 1)
    spread = jnp.broadcast_to(lengths[...].astype(jnp.float32), (64, 64))
    starts = jnp.sum(jnp.where(column_index < row_index, spread, 0.0), axis=1, keepdims=True)
    starts = jnp.sum(jnp.where(column_index == row_index, starts, 0.0), axis=0, keepdims=True)
    tokens = block * 128 + lax.broadcasted_iota(jnp.int32, (128, 64), 0)
    begin = jnp.max(jnp.where(starts <= tokens.astype(jnp.float32), starts, 0.0), axis=1, keepdims=True)
    begins[...] = jnp.broadcast_to(begin, (128, 128)).astype(jnp.int32)

    def mask(positions):
        token = block * 128 + lax.broadcasted_iota(jnp.int32, (128, 128), 0)
        seen = (positions >= begins[...]) & (positions <= token)
        bias[...] = jnp.where(seen, 0.0, HIDDEN)

    def take(group, source, chunk, first, last_results=None):
        index = lax.broadcasted_iota(jnp.int32, (128, 128), 1)
        slot = jnp.maximum(source, 0) * 2
        left = jnp.where(source >= 0, image_places[slot], -1)
        right = jnp.where(source >= 0, image_places[slot + 1], -1)
        mask(jnp.where(group == TEXT, source * 128 + index, jnp.where(index < 64, left, right)))
        kind = jnp.where(group == TEXT, 0, 1)
        attend(queries, chunks, bias, tops, totals, sums, kind, chunk, first, last_results)

    def send(source, target, sem, receive, device):
        return pltpu.make_async_remote_copy(
            src_ref=source,
            dst_ref=target,
            send_sem=send_sems.at[sem],
            recv_sem=receive,
            device_id=device,
            device_id_type=MESH,
        )

    def sources_of_own(group, sem):
        for part in range(2):
            for kind, (step, goes) in enumerate(((1, place <= 2), (3, (place >= 1) & ~last_row))):
                yield goes, send(
                    chunks.at[group + OWN, part],
                    chunks.at[group + place, part],
                    sem + 2 * part + kind,
                    recv_sems.at[group + place, part],
                    at(step, lane),
                )

    expected = pick(place, (3, 6, 6, 4)) - jnp.where(last_row & (place >= 1), 1, 0)
    expected = expected - jnp.where(first_row & ((place == 1) | (place == 2)), 1, 0)
    far_sources = pick(place, (2, 0, 0, 2)) - jnp.where(first_row & (place == 0), 2, 0)
    far_sources = far_sources + jnp.where(last_row & (place >= 2), 1, 0)
    pl.semaphore_wait(barrier, expected + jnp.where(half == 0, -1, far_sources))

    def invite(step, to_lane):
        pl.semaphore_signal(far_ready, inc=1, device_id=at(step, to_lane), device_id_type=MESH)

    @pl.when(half == 1)
    def _():
        for_far_sources(invite)

    own_near, own_far = NEAR + OWN, FAR + OWN
    swap_far = send(
        columns(other_far_lane), chunks.at[own_far, :, :, core], 0, recv_sems.at[own_far, 0], at(0, other_lane)
    )
    swap_near = send(
        columns(other_lane), chunks.at[own_near, :, :, core], 1, recv_sems.at[own_near, 0], at(0, other_lane)
    )
    swap_far.start()
    swap_near.start()

    def start(copies):
        for goes, copy in copies:

            @pl.when(goes)
            def _(copy=copy):
                copy.start()

    loads[0].wait()
    sent = list(sources_of_own(TEXT, 2))
    start(sent)
    loads[2].wait()
    swap_far.wait_recv()
    to_far = [
        send(
            chunks.at[own_far, part],
            chunks.at[FAR + place, part],
            6 + part,
            recv_sems.at[FAR + place, part],
            at(far_step, far_lane),
        )
        for part in range(2)
    ]
    @pl.when(half == 1)
    def _():
        for copy in to_far:
            copy.start()

    loads[1].wait()
    swap_near.wait_recv()
    sent_near = list(sources_of_own(NEAR, 8))
    start(sent_near)

    sent += sent_near
    loads[3].wait()
    take(TEXT, block, TEXT + OWN, True)

    @pl.when(half == 0)
    def _():
        pl.semaphore_wait(far_ready, 1)
        for copy in to_far:
            copy.start()

    loads[4].wait()
    take(NEAR, block, NEAR + OWN, True)

    taken, text_left, finished = 0, [ROW - 1] * ROW, False
    for number, (groups, sources, parts, steps, ready) in enumerate(plan()):
        group, source, part, step = (pick(place, table) for table in (groups, sources, parts, steps))
        chunk = group + source
        origin = block - place + source - jnp.where(source > place, ROW, 0)
        forward = send(
            chunks.at[chunk, part], chunks.at[chunk, part], 12 + number, recv_sems.at[chunk, part], at(step, lane)
        )
        goes = (origin >= 0) & (step != 0) & ~((step == 3) & last_row)
        @pl.when(origin >= 0)
        def _(forward=forward):
            forward.wait_recv()

        @pl.when(goes)
        def _(forward=forward):
            forward.start()

        sent.append((goes, forward))
        for whole_groups, whole_sources in ready:
            group, source = pick(place, whole_groups), pick(place, whole_sources)
            origin = block - place + source - jnp.where(source > place, ROW, 0)
            taken += 1
            last_results = results if taken == 10 else None

            @pl.when(origin >= 0)
            def _(group=group, source=source, origin=origin, last_results=last_results):
                take(group, origin, group + source, False, last_results)

            if last_results is not None:

                @pl.when(origin < 0)
                def _():
                    finish(results, totals, sums, 1)

            text_left = [left - (at_place == TEXT) for left, at_place in zip(text_left, whole_groups)]
            if not finished and max(text_left) == 0:
                finished = True
                finish(results, totals, sums, 0)

    swap_near.wait_send()
    swap_far.wait_send()
    for copy in to_far:
        copy.wait_send()
    for goes, copy in sent:

        @pl.when(goes)
        def _(copy=copy):
            copy.wait_send()


def per_device(self_queries, cross_queries, text_pairs, image_pairs, doc_lengths, image_places):
    anywhere = pl.BlockSpec(memory_space=pl.ANY)
    state = pltpu.VMEM((2, 2, 1024, HEAD_DIM), jnp.float32)
    results = pl.pallas_call(
        functools.partial(kernel, lax.axis_size("ctx")),
        out_shape=pltpu.VMEM((2, *self_queries.shape), jnp.bfloat16),
        in_specs=[anywhere] * 6,
        out_specs=pl.BlockSpec(memory_space=pltpu.VMEM),
        scratch_shapes=[
            pltpu.VMEM((1, 64), jnp.int32),
            pltpu.SMEM((256,), jnp.int32),
            pltpu.VMEM((2, 128, 2048), jnp.bfloat16),
            pltpu.VMEM((15, 2, 2, 2, 32, 256), jnp.bfloat16),
            pltpu.VMEM((128, 128), jnp.float32),
            pltpu.VMEM((128, 128), jnp.int32),
            state,
            state,
            state,
            pltpu.SemaphoreType.DMA((7,)),
            pltpu.SemaphoreType.DMA((12 + len(ORDER[0]),)),
            pltpu.SemaphoreType.DMA((15, 2)),
            pltpu.SemaphoreType.REGULAR,
        ],
        compiler_params=pltpu.CompilerParams(
            collective_id=0, has_side_effects=True, vmem_limit_bytes=60 << 20
        ),
    )(
        self_queries,
        cross_queries,
        text_pairs.reshape(2, 2, 2, 32, 256),
        image_pairs,
        doc_lengths.reshape(1, 64),
        image_places,
    )
    return results[0], results[1]


def solution(mesh):
    placed = (
        P("ctx", "tp"),
        P("ctx", "tp"),
        P(None, "ctx", "tp"),
        P(None, "ctx", "tp", None),
        P(),
        P(),
    )
    return jax.shard_map(
        per_device,
        mesh=mesh,
        in_specs=placed,
        out_specs=(P("ctx", "tp"), P("ctx", "tp")),
        check_vma=False,
    )
```

```python
import functools
import math
import jax
import jax.numpy as jnp
from jax import lax
from jax.experimental import pallas as pl
from jax.experimental.pallas import tpu as pltpu
from jax.sharding import PartitionSpec as P

HEAD_DIM = 128
ROW = 4
OWN = 4
TEXT, NEAR, FAR = 0, 5, 10
HIDDEN = -1e30
LOWEST = -1e29
EXPONENT = math.log2(math.e) / math.sqrt(HEAD_DIM)
MESH = pl.DeviceIdType.MESH

ORDER = (
    ("G3a", "G2a", "T2b", "G2b", "T1b", "I1a", "T1a", "G3b", "I2b", "I3a", "I1b", "T3b", "I3b", "T2a", "T3a", "I2a", "G0a", "G1b", "G1a", "G0b"),
    ("T0b", "T2a", "I0a", "I0b", "T2b", "I2a", "T0a", "T3b", "I2b", "G3a", "T3a", "I3a", "G2a", "I3b", "G2b", "G1b", "G3b", "G0a", "G1a", "G0b"),
    ("T1a", "I1a", "I1b", "T3a", "T1b", "T3b", "I3a", "T0b", "T0a", "I3b", "G0a", "I0a", "I0b", "G1b", "G0b", "G3a", "G1a", "G2a", "G3b", "G2b"),
    ("G0a", "G1b", "T1a", "G0b", "I2b", "I2a", "I1a", "G1a", "T0b", "T2b", "I1b", "T2a", "I0a", "T0a", "I0b", "G3a", "G2a", "T1b", "G3b", "G2b"),
)
CLASSES = {"T": TEXT, "I": NEAR, "G": FAR}
PARTS = {"a": 0, "b": 1}
FAR_ON = ((0, -1, -1, -1), (0, 3, -1, -1), (1, -3, 1, 0), (1, 1, -3, 0))


def onward(group, source, place):
    if group == FAR:
        return FAR_ON[source][place]
    if source < place:
        return 1 if place < ROW - 1 else 0
    return -1 if place > 0 else 0


def plan():
    orders = [[(CLASSES[word[0]], int(word[1]), PARTS[word[2]]) for word in order] for order in ORDER]
    whole = []
    for order in orders:
        seen, done = set(), []
        for number, (group, source, _) in enumerate(order):
            if (group, source) in seen:
                done.append((number, group, source))
            seen.add((group, source))
        whole.append(done)
    ready = [[] for _ in orders[0]]
    for entry in zip(*whole):
        ready[max(number for number, _, _ in entry)].append(
            (tuple(group for _, group, _ in entry), tuple(source for _, _, source in entry))
        )
    for number, entry in enumerate(zip(*orders)):
        groups, sources, parts = (tuple(column) for column in zip(*entry))
        steps = tuple(onward(groups[place], sources[place], place) for place in range(ROW))
        yield groups, sources, parts, steps, ready[number]


FAR_STEP = (3, 2, 2, 1)
FAR_STEP_LAST = (3, 2, 0, 0)


def pick(place, values):
    result = jnp.int32(values[-1])
    for index, value in enumerate(values[:-1]):
        result = jnp.where(place == index, value, result)
    return result


def normalized(weighted, totals):
    total = jnp.sum(totals, axis=1, keepdims=True)
    positive = total > 0.0
    inverse = jnp.where(positive, 1.0 / jnp.where(positive, total, 1.0), 0.0)
    return (weighted * inverse).astype(jnp.bfloat16)


def attend(queries, chunks, bias, tops, totals, sums, kind, chunk, first, results=None):
    for group in range(2):
        columns = slice(group * HEAD_DIM, (group + 1) * HEAD_DIM)
        keys = chunks[chunk, 0, :, :, :, columns].reshape(HEAD_DIM, HEAD_DIM)
        values = chunks[chunk, 1, :, :, :, columns].reshape(HEAD_DIM, HEAD_DIM)
        heads = [queries[kind, :, h * HEAD_DIM : (h + 1) * HEAD_DIM] for h in range(group * 8, group * 8 + 8)]
        stacked = jnp.concatenate(heads, axis=0)
        scores = lax.dot_general(stacked, keys, (((1,), (1,)), ((), ())), preferred_element_type=jnp.float32)
        scores = (scores.reshape(8, 128, 128) + bias[...][None]).reshape(1024, 128)
        top = jnp.max(scores, axis=1, keepdims=True)
        if first:
            new_top = jnp.broadcast_to(jnp.maximum(top, LOWEST), (1024, 128))
            weights = jnp.exp2((scores - new_top) * EXPONENT)
            total = weights
            weighted = jnp.dot(weights.astype(jnp.bfloat16), values, preferred_element_type=jnp.float32)
        else:
            old_top = tops[kind, group]
            new_top = jnp.maximum(old_top, top)
            weights = jnp.exp2((scores - new_top) * EXPONENT)
            factor = jnp.exp2((old_top - new_top) * EXPONENT)
            total = totals[kind, group] * factor + weights
            weighted = sums[kind, group] * factor + jnp.dot(
                weights.astype(jnp.bfloat16), values, preferred_element_type=jnp.float32
            )
        if results is not None:
            scaled = normalized(weighted, total)
            for head in range(8):
                columns = slice((group * 8 + head) * HEAD_DIM, (group * 8 + head + 1) * HEAD_DIM)
                results[1, :, columns] = scaled[head * 128 : (head + 1) * 128]
            continue
        tops[kind, group] = new_top
        totals[kind, group] = total
        sums[kind, group] = weighted


def finish(results, totals, sums, kind):
    for head in range(16):
        rows = slice((head % 8) * 128, (head % 8 + 1) * 128)
        scaled = normalized(sums[kind, head // 8, rows, :], totals[kind, head // 8, rows, :])
        results[kind, :, head * HEAD_DIM : (head + 1) * HEAD_DIM] = scaled


def kernel(
    blocks,
    self_queries,
    cross_queries,
    text,
    images,
    lengths_hbm,
    places_hbm,
    results,
    lengths,
    image_places,
    queries,
    chunks,
    bias,
    begins,
    tops,
    totals,
    sums,
    local_sems,
    send_sems,
    recv_sems,
    far_ready,
):
    block = lax.axis_index("ctx")
    lane = lax.axis_index("tp")
    place = lax.rem(block, ROW)
    core = lax.rem(lane, 2)
    other_lane = lane + 1 - 2 * core
    far_lane = lax.rem(lane + 2, 4)
    other_far_lane = lax.rem(other_lane + 2, 4)

    def at(step, to_lane):
        return (lax.rem(block + step + blocks, blocks), to_lane)

    half = lane // 2
    first_row = block < ROW
    last_row = block >= blocks - ROW

    barrier = pltpu.get_barrier_semaphore()

    def greet(step, to_lane):
        pl.semaphore_signal(barrier, inc=1, device_id=at(step, to_lane), device_id_type=MESH)

    greet(0, other_lane)

    @pl.when(place >= 1)
    def _():
        greet(-1, lane)

    @pl.when(place <= 2)
    def _():
        greet(1, lane)

    @pl.when((place <= 2) & ~first_row)
    def _():
        greet(-3, lane)

    @pl.when((place >= 2) & ~last_row)
    def _():
        greet(3, lane)

    far_step = jnp.where(last_row, pick(place, FAR_STEP_LAST), pick(place, FAR_STEP))

    @pl.when(half == 0)
    def _():
        greet(far_step, far_lane)

    def for_far_sources(tell):
        @pl.when((place >= 2) & last_row)
        def _():
            tell(0, far_lane)

        @pl.when((place == 0) & ~first_row)
        def _():
            tell(-1, far_lane)
            tell(-2, far_lane)

        @pl.when(place == 3)
        def _():
            tell(-3, far_lane)
            tell(-2, far_lane)

    @pl.when(half == 0)
    def _():
        for_far_sources(greet)

    def columns(of_lane):
        return images.at[:, :, :, pl.ds(pl.multiple_of(of_lane * 256, 256), 256)]

    loads = [
        pltpu.make_async_copy(text, chunks.at[TEXT + OWN], local_sems.at[0]),
        pltpu.make_async_copy(columns(lane), chunks.at[NEAR + OWN, :, :, core], local_sems.at[1]),
        pltpu.make_async_copy(columns(far_lane), chunks.at[FAR + OWN, :, :, core], local_sems.at[2]),
        pltpu.make_async_copy(self_queries, queries.at[0], local_sems.at[3]),
        pltpu.make_async_copy(cross_queries, queries.at[1], local_sems.at[4]),
        pltpu.make_async_copy(lengths_hbm, lengths, local_sems.at[5]),
        pltpu.make_async_copy(places_hbm, image_places, local_sems.at[6]),
    ]
    for load in loads:
        load.start()

    loads[5].wait()
    loads[6].wait()

    row_index = lax.broadcasted_iota(jnp.int32, (64, 64), 0)
    column_index = lax.broadcasted_iota(jnp.int32, (64, 64), 1)
    spread = jnp.broadcast_to(lengths[...].astype(jnp.float32), (64, 64))
    starts = jnp.sum(jnp.where(column_index < row_index, spread, 0.0), axis=1, keepdims=True)
    starts = jnp.sum(jnp.where(column_index == row_index, starts, 0.0), axis=0, keepdims=True)
    tokens = block * 128 + lax.broadcasted_iota(jnp.int32, (128, 64), 0)
    begin = jnp.max(jnp.where(starts <= tokens.astype(jnp.float32), starts, 0.0), axis=1, keepdims=True)
    begins[...] = jnp.broadcast_to(begin, (128, 128)).astype(jnp.int32)

    def mask(positions):
        token = block * 128 + lax.broadcasted_iota(jnp.int32, (128, 128), 0)
        seen = (positions >= begins[...]) & (positions <= token)
        bias[...] = jnp.where(seen, 0.0, HIDDEN)

    def take(group, source, chunk, first, last_results=None):
        index = lax.broadcasted_iota(jnp.int32, (128, 128), 1)
        slot = jnp.maximum(source, 0) * 2
        left = jnp.where(source >= 0, image_places[slot], -1)
        right = jnp.where(source >= 0, image_places[slot + 1], -1)
        mask(jnp.where(group == TEXT, source * 128 + index, jnp.where(index < 64, left, right)))
        kind = jnp.where(group == TEXT, 0, 1)
        attend(queries, chunks, bias, tops, totals, sums, kind, chunk, first, last_results)

    def send(source, target, sem, receive, device):
        return pltpu.make_async_remote_copy(
            src_ref=source,
            dst_ref=target,
            send_sem=send_sems.at[sem],
            recv_sem=receive,
            device_id=device,
            device_id_type=MESH,
        )

    def sources_of_own(group, sem):
        for part in range(2):
            for kind, (step, goes) in enumerate(((1, place <= 2), (3, (place >= 1) & ~last_row))):
                yield goes, send(
                    chunks.at[group + OWN, part],
                    chunks.at[group + place, part],
                    sem + 2 * part + kind,
                    recv_sems.at[group + place, part],
                    at(step, lane),
                )

    expected = pick(place, (3, 6, 6, 4)) - jnp.where(last_row & (place >= 1), 1, 0)
    expected = expected - jnp.where(first_row & ((place == 1) | (place == 2)), 1, 0)
    far_sources = pick(place, (2, 0, 0, 2)) - jnp.where(first_row & (place == 0), 2, 0)
    far_sources = far_sources + jnp.where(last_row & (place >= 2), 1, 0)
    pl.semaphore_wait(barrier, expected + jnp.where(half == 0, -1, far_sources))

    def invite(step, to_lane):
        pl.semaphore_signal(far_ready, inc=1, device_id=at(step, to_lane), device_id_type=MESH)

    @pl.when(half == 1)
    def _():
        for_far_sources(invite)

    own_near, own_far = NEAR + OWN, FAR + OWN
    swap_far = send(
        columns(other_far_lane), chunks.at[own_far, :, :, core], 0, recv_sems.at[own_far, 0], at(0, other_lane)
    )
    swap_near = send(
        columns(other_lane), chunks.at[own_near, :, :, core], 1, recv_sems.at[own_near, 0], at(0, other_lane)
    )
    swap_far.start()
    swap_near.start()

    def start(copies):
        for goes, copy in copies:

            @pl.when(goes)
            def _(copy=copy):
                copy.start()

    loads[0].wait()
    sent = list(sources_of_own(TEXT, 2))
    start(sent)
    loads[2].wait()
    swap_far.wait_recv()
    to_far = [
        send(
            chunks.at[own_far, part],
            chunks.at[FAR + place, part],
            6 + part,
            recv_sems.at[FAR + place, part],
            at(far_step, far_lane),
        )
        for part in range(2)
    ]
    @pl.when(half == 1)
    def _():
        for copy in to_far:
            copy.start()

    loads[1].wait()
    swap_near.wait_recv()
    sent_near = list(sources_of_own(NEAR, 8))
    start(sent_near)

    sent += sent_near
    loads[3].wait()
    take(TEXT, block, TEXT + OWN, True)

    @pl.when(half == 0)
    def _():
        pl.semaphore_wait(far_ready, 1)
        for copy in to_far:
            copy.start()

    loads[4].wait()
    take(NEAR, block, NEAR + OWN, True)

    taken, text_left, finished = 0, [ROW - 1] * ROW, False
    for number, (groups, sources, parts, steps, ready) in enumerate(plan()):
        group, source, part, step = (pick(place, table) for table in (groups, sources, parts, steps))
        chunk = group + source
        origin = block - place + source - jnp.where(source > place, ROW, 0)
        forward = send(
            chunks.at[chunk, part], chunks.at[chunk, part], 12 + number, recv_sems.at[chunk, part], at(step, lane)
        )
        goes = (origin >= 0) & (step != 0) & ~((step == 3) & last_row)
        @pl.when(origin >= 0)
        def _(forward=forward):
            forward.wait_recv()

        @pl.when(goes)
        def _(forward=forward):
            forward.start()

        sent.append((goes, forward))
        for whole_groups, whole_sources in ready:
            group, source = pick(place, whole_groups), pick(place, whole_sources)
            origin = block - place + source - jnp.where(source > place, ROW, 0)
            taken += 1
            last_results = results if taken == 10 else None

            @pl.when(origin >= 0)
            def _(group=group, source=source, origin=origin, last_results=last_results):
                take(group, origin, group + source, False, last_results)

            if last_results is not None:

                @pl.when(origin < 0)
                def _():
                    finish(results, totals, sums, 1)

            text_left = [left - (at_place == TEXT) for left, at_place in zip(text_left, whole_groups)]
            if not finished and max(text_left) == 0:
                finished = True
                finish(results, totals, sums, 0)

    swap_near.wait_send()
    swap_far.wait_send()
    for copy in to_far:
        copy.wait_send()
    for goes, copy in sent:

        @pl.when(goes)
        def _(copy=copy):
            copy.wait_send()


def per_device(self_queries, cross_queries, text_pairs, image_pairs, doc_lengths, image_places):
    anywhere = pl.BlockSpec(memory_space=pl.ANY)
    state = pltpu.VMEM((2, 2, 1024, HEAD_DIM), jnp.float32)
    results = pl.pallas_call(
        functools.partial(kernel, lax.axis_size("ctx")),
        out_shape=pltpu.VMEM((2, *self_queries.shape), jnp.bfloat16),
        in_specs=[anywhere] * 6,
        out_specs=pl.BlockSpec(memory_space=pltpu.VMEM),
        scratch_shapes=[
            pltpu.VMEM((1, 64), jnp.int32),
            pltpu.SMEM((256,), jnp.int32),
            pltpu.VMEM((2, 128, 2048), jnp.bfloat16),
            pltpu.VMEM((15, 2, 2, 2, 32, 256), jnp.bfloat16),
            pltpu.VMEM((128, 128), jnp.float32),
            pltpu.VMEM((128, 128), jnp.int32),
            state,
            state,
            state,
            pltpu.SemaphoreType.DMA((7,)),
            pltpu.SemaphoreType.DMA((12 + len(ORDER[0]),)),
            pltpu.SemaphoreType.DMA((15, 2)),
            pltpu.SemaphoreType.REGULAR,
        ],
        compiler_params=pltpu.CompilerParams(
            collective_id=0, has_side_effects=True, vmem_limit_bytes=60 << 20
        ),
    )(
        self_queries,
        cross_queries,
        text_pairs.reshape(2, 2, 2, 32, 256),
        image_pairs,
        doc_lengths.reshape(1, 64),
        image_places,
    )
    return results[0], results[1]


def solution(mesh):
    placed = (
        P("ctx", "tp"),
        P("ctx", "tp"),
        P(None, "ctx", "tp"),
        P(None, "ctx", "tp", None),
        P(),
        P(),
    )
    return jax.shard_map(
        per_device,
        mesh=mesh,
        in_specs=placed,
        out_specs=(P("ctx", "tp"), P("ctx", "tp")),
        check_vma=False,
    )
```

```python
import functools
import math
import jax
import jax.numpy as jnp
from jax import lax
from jax.experimental import pallas as pl
from jax.experimental.pallas import tpu as pltpu
from jax.sharding import PartitionSpec as P

HEAD_DIM = 128
ROW = 4
OWN = 4
TEXT, NEAR, FAR = 0, 5, 10
HIDDEN = -1e30
LOWEST = -1e29
EXPONENT = math.log2(math.e) / math.sqrt(HEAD_DIM)
MESH = pl.DeviceIdType.MESH

ORDER = (
    ("G3a", "G2a", "T2b", "G2b", "T1b", "I1a", "T1a", "G3b", "I2b", "I3a", "I1b", "T3b", "I3b", "T2a", "T3a", "I2a", "G0a", "G1b", "G1a", "G0b"),
    ("T0b", "T2a", "I0a", "I0b", "T2b", "I2a", "T0a", "T3b", "I2b", "G3a", "T3a", "I3a", "G2a", "I3b", "G2b", "G1b", "G3b", "G0a", "G1a", "G0b"),
    ("T1a", "I1a", "I1b", "T3a", "T1b", "T3b", "I3a", "T0b", "T0a", "I3b", "G0a", "I0a", "I0b", "G1b", "G0b", "G3a", "G1a", "G2a", "G3b", "G2b"),
    ("G0a", "G1b", "T1a", "G0b", "I2b", "I2a", "I1a", "G1a", "T0b", "T2b", "I1b", "T2a", "I0a", "T0a", "I0b", "G3a", "G2a", "T1b", "G3b", "G2b"),
)
CLASSES = {"T": TEXT, "I": NEAR, "G": FAR}
PARTS = {"a": 0, "b": 1}
FAR_ON = ((0, -1, -1, -1), (0, 3, -1, -1), (1, -3, 1, 0), (1, 1, -3, 0))


def onward(group, source, place):
    if group == FAR:
        return FAR_ON[source][place]
    if source < place:
        return 1 if place < ROW - 1 else 0
    return -1 if place > 0 else 0


def plan():
    orders = [[(CLASSES[word[0]], int(word[1]), PARTS[word[2]]) for word in order] for order in ORDER]
    whole = []
    for order in orders:
        seen, done = set(), []
        for number, (group, source, _) in enumerate(order):
            if (group, source) in seen:
                done.append((number, group, source))
            seen.add((group, source))
        whole.append(done)
    ready = [[] for _ in orders[0]]
    for entry in zip(*whole):
        ready[max(number for number, _, _ in entry)].append(
            (tuple(group for _, group, _ in entry), tuple(source for _, _, source in entry))
        )
    for number, entry in enumerate(zip(*orders)):
        groups, sources, parts = (tuple(column) for column in zip(*entry))
        steps = tuple(onward(groups[place], sources[place], place) for place in range(ROW))
        yield groups, sources, parts, steps, ready[number]


FAR_STEP = (3, 2, 2, 1)
FAR_STEP_LAST = (3, 2, 0, 0)


def pick(place, values):
    result = jnp.int32(values[-1])
    for index, value in enumerate(values[:-1]):
        result = jnp.where(place == index, value, result)
    return result


def normalized(weighted, totals):
    total = jnp.sum(totals, axis=1, keepdims=True)
    positive = total > 0.0
    inverse = jnp.where(positive, 1.0 / jnp.where(positive, total, 1.0), 0.0)
    return (weighted * inverse).astype(jnp.bfloat16)


def attend(queries, chunks, bias, tops, totals, sums, kind, chunk, first, results=None):
    for group in range(2):
        columns = slice(group * HEAD_DIM, (group + 1) * HEAD_DIM)
        keys = chunks[chunk, 0, :, :, :, columns].reshape(HEAD_DIM, HEAD_DIM)
        values = chunks[chunk, 1, :, :, :, columns].reshape(HEAD_DIM, HEAD_DIM)
        heads = [queries[kind, :, h * HEAD_DIM : (h + 1) * HEAD_DIM] for h in range(group * 8, group * 8 + 8)]
        stacked = jnp.concatenate(heads, axis=0)
        scores = lax.dot_general(stacked, keys, (((1,), (1,)), ((), ())), preferred_element_type=jnp.float32)
        scores = (scores.reshape(8, 128, 128) + bias[...][None]).reshape(1024, 128)
        top = jnp.max(scores, axis=1, keepdims=True)
        if first:
            new_top = jnp.broadcast_to(jnp.maximum(top, LOWEST), (1024, 128))
            weights = jnp.exp2((scores - new_top) * EXPONENT)
            total = weights
            weighted = jnp.dot(weights.astype(jnp.bfloat16), values, preferred_element_type=jnp.float32)
        else:
            old_top = tops[kind, group]
            new_top = jnp.maximum(old_top, top)
            weights = jnp.exp2((scores - new_top) * EXPONENT)
            factor = jnp.exp2((old_top - new_top) * EXPONENT)
            total = totals[kind, group] * factor + weights
            weighted = sums[kind, group] * factor + jnp.dot(
                weights.astype(jnp.bfloat16), values, preferred_element_type=jnp.float32
            )
        if results is not None:
            scaled = normalized(weighted, total)
            for head in range(8):
                columns = slice((group * 8 + head) * HEAD_DIM, (group * 8 + head + 1) * HEAD_DIM)
                results[1, :, columns] = scaled[head * 128 : (head + 1) * 128]
            continue
        tops[kind, group] = new_top
        totals[kind, group] = total
        sums[kind, group] = weighted


def finish(results, totals, sums, kind):
    for head in range(16):
        rows = slice((head % 8) * 128, (head % 8 + 1) * 128)
        scaled = normalized(sums[kind, head // 8, rows, :], totals[kind, head // 8, rows, :])
        results[kind, :, head * HEAD_DIM : (head + 1) * HEAD_DIM] = scaled


def kernel(
    blocks,
    self_queries,
    cross_queries,
    text,
    images,
    lengths_hbm,
    places_hbm,
    results,
    lengths,
    image_places,
    queries,
    chunks,
    bias,
    begins,
    tops,
    totals,
    sums,
    local_sems,
    send_sems,
    recv_sems,
    far_ready,
):
    block = lax.axis_index("ctx")
    lane = lax.axis_index("tp")
    place = lax.rem(block, ROW)
    core = lax.rem(lane, 2)
    other_lane = lane + 1 - 2 * core
    far_lane = lax.rem(lane + 2, 4)
    other_far_lane = lax.rem(other_lane + 2, 4)

    def at(step, to_lane):
        return (lax.rem(block + step + blocks, blocks), to_lane)

    half = lane // 2
    first_row = block < ROW
    last_row = block >= blocks - ROW

    barrier = pltpu.get_barrier_semaphore()

    def greet(step, to_lane):
        pl.semaphore_signal(barrier, inc=1, device_id=at(step, to_lane), device_id_type=MESH)

    greet(0, other_lane)

    @pl.when(place >= 1)
    def _():
        greet(-1, lane)

    @pl.when(place <= 2)
    def _():
        greet(1, lane)

    @pl.when((place <= 2) & ~first_row)
    def _():
        greet(-3, lane)

    @pl.when((place >= 2) & ~last_row)
    def _():
        greet(3, lane)

    far_step = jnp.where(last_row, pick(place, FAR_STEP_LAST), pick(place, FAR_STEP))

    @pl.when(half == 0)
    def _():
        greet(far_step, far_lane)

    def for_far_sources(tell):
        @pl.when((place >= 2) & last_row)
        def _():
            tell(0, far_lane)

        @pl.when((place == 0) & ~first_row)
        def _():
            tell(-1, far_lane)
            tell(-2, far_lane)

        @pl.when(place == 3)
        def _():
            tell(-3, far_lane)
            tell(-2, far_lane)

    @pl.when(half == 0)
    def _():
        for_far_sources(greet)

    def columns(of_lane):
        return images.at[:, :, :, pl.ds(pl.multiple_of(of_lane * 256, 256), 256)]

    loads = [
        pltpu.make_async_copy(text, chunks.at[TEXT + OWN], local_sems.at[0]),
        pltpu.make_async_copy(columns(lane), chunks.at[NEAR + OWN, :, :, core], local_sems.at[1]),
        pltpu.make_async_copy(columns(far_lane), chunks.at[FAR + OWN, :, :, core], local_sems.at[2]),
        pltpu.make_async_copy(self_queries, queries.at[0], local_sems.at[3]),
        pltpu.make_async_copy(cross_queries, queries.at[1], local_sems.at[4]),
        pltpu.make_async_copy(lengths_hbm, lengths, local_sems.at[5]),
        pltpu.make_async_copy(places_hbm, image_places, local_sems.at[6]),
    ]
    for load in loads:
        load.start()

    loads[5].wait()
    loads[6].wait()

    row_index = lax.broadcasted_iota(jnp.int32, (64, 64), 0)
    column_index = lax.broadcasted_iota(jnp.int32, (64, 64), 1)
    spread = jnp.broadcast_to(lengths[...].astype(jnp.float32), (64, 64))
    starts = jnp.sum(jnp.where(column_index < row_index, spread, 0.0), axis=1, keepdims=True)
    starts = jnp.sum(jnp.where(column_index == row_index, starts, 0.0), axis=0, keepdims=True)
    tokens = block * 128 + lax.broadcasted_iota(jnp.int32, (128, 64), 0)
    begin = jnp.max(jnp.where(starts <= tokens.astype(jnp.float32), starts, 0.0), axis=1, keepdims=True)
    begins[...] = jnp.broadcast_to(begin, (128, 128)).astype(jnp.int32)

    def mask(positions):
        token = block * 128 + lax.broadcasted_iota(jnp.int32, (128, 128), 0)
        seen = (positions >= begins[...]) & (positions <= token)
        bias[...] = jnp.where(seen, 0.0, HIDDEN)

    def take(group, source, chunk, first, last_results=None):
        index = lax.broadcasted_iota(jnp.int32, (128, 128), 1)
        slot = jnp.maximum(source, 0) * 2
        left = jnp.where(source >= 0, image_places[slot], -1)
        right = jnp.where(source >= 0, image_places[slot + 1], -1)
        mask(jnp.where(group == TEXT, source * 128 + index, jnp.where(index < 64, left, right)))
        kind = jnp.where(group == TEXT, 0, 1)
        attend(queries, chunks, bias, tops, totals, sums, kind, chunk, first, last_results)

    def send(source, target, sem, receive, device):
        return pltpu.make_async_remote_copy(
            src_ref=source,
            dst_ref=target,
            send_sem=send_sems.at[sem],
            recv_sem=receive,
            device_id=device,
            device_id_type=MESH,
        )

    def sources_of_own(group, sem):
        for kind, (step, goes) in enumerate(((1, place <= 2), (3, (place >= 1) & ~last_row))):
            for part in range(2):
                yield goes, send(
                    chunks.at[group + OWN, part],
                    chunks.at[group + place, part],
                    sem + 2 * part + kind,
                    recv_sems.at[group + place, part],
                    at(step, lane),
                )

    expected = pick(place, (3, 6, 6, 4)) - jnp.where(last_row & (place >= 1), 1, 0)
    expected = expected - jnp.where(first_row & ((place == 1) | (place == 2)), 1, 0)
    far_sources = pick(place, (2, 0, 0, 2)) - jnp.where(first_row & (place == 0), 2, 0)
    far_sources = far_sources + jnp.where(last_row & (place >= 2), 1, 0)
    pl.semaphore_wait(barrier, expected + jnp.where(half == 0, -1, far_sources))

    def invite(step, to_lane):
        pl.semaphore_signal(far_ready, inc=1, device_id=at(step, to_lane), device_id_type=MESH)

    @pl.when(half == 1)
    def _():
        for_far_sources(invite)

    own_near, own_far = NEAR + OWN, FAR + OWN
    swap_far = send(
        columns(other_far_lane), chunks.at[own_far, :, :, core], 0, recv_sems.at[own_far, 0], at(0, other_lane)
    )
    swap_near = send(
        columns(other_lane), chunks.at[own_near, :, :, core], 1, recv_sems.at[own_near, 0], at(0, other_lane)
    )
    swap_far.start()
    swap_near.start()

    def start(copies):
        for goes, copy in copies:

            @pl.when(goes)
            def _(copy=copy):
                copy.start()

    loads[0].wait()
    sent = list(sources_of_own(TEXT, 2))
    start(sent)
    loads[2].wait()
    swap_far.wait_recv()
    to_far = [
        send(
            chunks.at[own_far, part],
            chunks.at[FAR + place, part],
            6 + part,
            recv_sems.at[FAR + place, part],
            at(far_step, far_lane),
        )
        for part in range(2)
    ]
    @pl.when(half == 1)
    def _():
        for copy in to_far:
            copy.start()

    loads[1].wait()
    swap_near.wait_recv()
    sent_near = list(sources_of_own(NEAR, 8))
    start(sent_near)

    sent += sent_near
    loads[3].wait()
    take(TEXT, block, TEXT + OWN, True)

    @pl.when(half == 0)
    def _():
        pl.semaphore_wait(far_ready, 1)
        for copy in to_far:
            copy.start()

    loads[4].wait()
    take(NEAR, block, NEAR + OWN, True)

    taken, text_left, finished = 0, [ROW - 1] * ROW, False
    for number, (groups, sources, parts, steps, ready) in enumerate(plan()):
        group, source, part, step = (pick(place, table) for table in (groups, sources, parts, steps))
        chunk = group + source
        origin = block - place + source - jnp.where(source > place, ROW, 0)
        forward = send(
            chunks.at[chunk, part], chunks.at[chunk, part], 12 + number, recv_sems.at[chunk, part], at(step, lane)
        )
        goes = (origin >= 0) & (step != 0) & ~((step == 3) & last_row)
        @pl.when(origin >= 0)
        def _(forward=forward):
            forward.wait_recv()

        @pl.when(goes)
        def _(forward=forward):
            forward.start()

        sent.append((goes, forward))
        for whole_groups, whole_sources in ready:
            group, source = pick(place, whole_groups), pick(place, whole_sources)
            origin = block - place + source - jnp.where(source > place, ROW, 0)
            taken += 1
            last_results = results if taken == 10 else None

            @pl.when(origin >= 0)
            def _(group=group, source=source, origin=origin, last_results=last_results):
                take(group, origin, group + source, False, last_results)

            if last_results is not None:

                @pl.when(origin < 0)
                def _():
                    finish(results, totals, sums, 1)

            text_left = [left - (at_place == TEXT) for left, at_place in zip(text_left, whole_groups)]
            if not finished and max(text_left) == 0:
                finished = True
                finish(results, totals, sums, 0)

    swap_near.wait_send()
    swap_far.wait_send()
    for copy in to_far:
        copy.wait_send()
    for goes, copy in sent:

        @pl.when(goes)
        def _(copy=copy):
            copy.wait_send()


def per_device(self_queries, cross_queries, text_pairs, image_pairs, doc_lengths, image_places):
    anywhere = pl.BlockSpec(memory_space=pl.ANY)
    state = pltpu.VMEM((2, 2, 1024, HEAD_DIM), jnp.float32)
    results = pl.pallas_call(
        functools.partial(kernel, lax.axis_size("ctx")),
        out_shape=pltpu.VMEM((2, *self_queries.shape), jnp.bfloat16),
        in_specs=[anywhere] * 6,
        out_specs=pl.BlockSpec(memory_space=pltpu.VMEM),
        scratch_shapes=[
            pltpu.VMEM((1, 64), jnp.int32),
            pltpu.SMEM((256,), jnp.int32),
            pltpu.VMEM((2, 128, 2048), jnp.bfloat16),
            pltpu.VMEM((15, 2, 2, 2, 32, 256), jnp.bfloat16),
            pltpu.VMEM((128, 128), jnp.float32),
            pltpu.VMEM((128, 128), jnp.int32),
            state,
            state,
            state,
            pltpu.SemaphoreType.DMA((7,)),
            pltpu.SemaphoreType.DMA((12 + len(ORDER[0]),)),
            pltpu.SemaphoreType.DMA((15, 2)),
            pltpu.SemaphoreType.REGULAR,
        ],
        compiler_params=pltpu.CompilerParams(
            collective_id=0, has_side_effects=True, vmem_limit_bytes=60 << 20
        ),
    )(
        self_queries,
        cross_queries,
        text_pairs.reshape(2, 2, 2, 32, 256),
        image_pairs,
        doc_lengths.reshape(1, 64),
        image_places,
    )
    return results[0], results[1]


def solution(mesh):
    placed = (
        P("ctx", "tp"),
        P("ctx", "tp"),
        P(None, "ctx", "tp"),
        P(None, "ctx", "tp", None),
        P(),
        P(),
    )
    return jax.shard_map(
        per_device,
        mesh=mesh,
        in_specs=placed,
        out_specs=(P("ctx", "tp"), P("ctx", "tp")),
        check_vma=False,
    )
```
